256 devices in a mesh: cache: 16 (over x, y), proj: 16 (over z, core).
Axes of the slice: x: 4, y: 4, z: 8, core: 2. Of those that a mesh axis runs over, the one named last changes fastest.
Arguments:
- compressed_query: bfloat16 [128, 1536], replicated, may hold values from -6 to 6
- query_gain: float32 [1536], replicated, may hold values from 0.25 to 1.75
- w_query: bfloat16 [1536, 24576], P('cache', 'proj'), may hold values from -0.15625 to 0.15625
- w_key: bfloat16 [128, 128, 512], P('proj'), may hold values from -0.5 to 0.5
- value_up_weight: bfloat16 [128, 512, 128], P('proj'), may hold values from -0.25 to 0.25
- w_output: bfloat16 [16384, 7168], P('proj', 'cache'), may hold values from -0.046875 to 0.046875
- latent_cache: bfloat16 [128, 16384, 576], P('proj', 'cache'), may hold values from -700 to 700
- context_lengths: int32 [128], replicated, may hold values from 8192 to 16384
- block_ids: int32 [128, 32], P('proj'), may hold values from -1 to 255, as said below
- block_counts: int32 [128], P('proj'), may hold values from 8 to 32
Outputs:
- attention_out: bfloat16 [128, 7168], P('proj', 'cache')
The draws below stay inside these ranges and needn't reach their ends.
Inputs may be any that keep to these rules, and one draw needn't show every extreme that they name: `block_ids`: the first block_counts[r] entries of row r are distinct blocks of 64 positions that start before context_lengths[r], the first of them holding position context_lengths[r] - 1; the other entries are -1. At most 4 listed blocks of a row lie within one run of 1024 positions that starts at a multiple of 1024, and some row has exactly 4 in one such run.
All inputs are finite; a program needn't handle non-finite values.
Results may differ from the reference program's by a relative error of at most 0.027.
The reference program's roundings to bfloat16 on the way count: a program that leaves them out, or rounds other values in their place, can miss the bound.
Values may be sent and summed in bfloat16 or wider, within the bound.
A program may use at most 128 MiB of HBM per device.

```python
import jax
import jax.numpy as jnp
from jax import lax

D = 7168
QR = 1536
H = 128
NOPE = 128
ROPE = 64
KVR = 512
VD = 128
NSEL = 32
BLK = 64
CTX_DEV = 1024
ROWS = 128
CTX = 16384


def select_blocks(key):
    key = jax.random.fold_in(key, 101)
    first_key, second_key, third_key = jax.random.split(key, 3)
    lengths = jax.random.randint(first_key, (ROWS,), CTX // 2, CTX + 1)
    lengths = lengths.at[0].set(CTX).at[1].set(CTX // 2)
    counts = jax.random.randint(second_key, (ROWS,), NSEL // 4, NSEL + 1)
    counts = counts.at[0].set(NSEL).at[1].set(NSEL // 4)
    blocks = CTX // BLK
    per_shard = CTX_DEV // BLK
    shards = CTX // CTX_DEV
    bound = max(2, 2 * NSEL // shards)
    bits = jax.random.randint(third_key, (ROWS, blocks), 0, 2 ** 16)
    index = jnp.arange(blocks, dtype=jnp.int32)
    sorted_segments = bits * blocks + index[None, :]
    have = (lengths + BLK - 1) // BLK
    sorted_segments = jnp.where(index[None, :] >= have[:, None], -1, sorted_segments)
    sorted_segments = jnp.where(index[None, :] == (have - 1)[:, None], 2 ** 27, sorted_segments)
    grouped = sorted_segments.reshape(ROWS, shards, per_shard)
    order = jnp.argsort(-grouped, axis=-1, stable=True)
    inner_rank = jnp.argsort(order, axis=-1, stable=True).reshape(ROWS, blocks)
    retained_segments = (inner_rank < bound) & (sorted_segments >= 0)
    holder_partition = index // per_shard
    final_partition = (have - 1) // per_shard
    preference_increment = jnp.where(holder_partition[None, :] == final_partition[:, None], 2 ** 28, 0)
    segment_preference = jnp.where(retained_segments, sorted_segments + preference_increment, -1)
    picked = lax.top_k(segment_preference, NSEL)[1].astype(jnp.int32)
    slots = jnp.arange(NSEL, dtype=jnp.int32)[None, :]
    picked = jnp.where(slots < counts[:, None], picked, -1)
    return (lengths.astype(jnp.int32), counts.astype(jnp.int32), picked)


def draw_context_lengths(key, part):
    return select_blocks(key)[0]


def draw_block_counts(key, part):
    return select_blocks(key)[1]


def draw_block_ids(key, part):
    return select_blocks(key)[2]


def draw_latent_cache(key, part):
    key = jax.random.fold_in(key, 7)
    base_key = jax.random.fold_in(key, 0)
    shape = (ROWS, CTX, KVR + ROPE)
    base = jnp.clip(jax.random.normal(base_key, shape, jnp.float32), -6.0, 6.0)
    return base.astype(jnp.bfloat16)


def block_scale(rng, shape, cuts, smallest, high):
    level, own = 1.0, jax.random.fold_in(rng, 6)
    for axis_at, blocks in cuts:
        heights = jnp.exp(jax.random.uniform(jax.random.fold_in(own, axis_at), (blocks,), jnp.float32, smallest / len(cuts), high / len(cuts)))
        level = level * jnp.repeat(heights, shape[axis_at] // blocks).reshape([-1 if axis == axis_at else 1 for axis in range(len(shape))])
    return level


def gaussian(own_key, shape, deviation, most, cuts=(), kind=jnp.bfloat16):
    drawn = deviation * jax.random.normal(own_key, shape, jnp.float32)
    if cuts:
        drawn = drawn * block_scale(own_key, shape, cuts, -0.22, 0.18)
    return jnp.clip(drawn, -most, most).astype(kind)


def setup_inputs(seed: int = 0) -> dict:
    seeds = jax.random.split(jax.random.key(seed), 11)
    return {
        "compressed_query": gaussian(seeds[0], (ROWS, QR), 1.0, 6.0),
        "query_gain": jnp.clip(1.0 + 0.15 * jax.random.normal(seeds[1], (QR,), jnp.float32), 0.25, 1.75),
        "w_query": gaussian(seeds[2], (QR, H * (NOPE + ROPE)), QR ** -0.5, 0.15625, ((0, 16), (1, 16))),
        "w_key": gaussian(seeds[3], (H, NOPE, KVR), NOPE ** -0.5, 0.5, ((0, 16),)),
        "value_up_weight": gaussian(seeds[4], (H, KVR, VD), KVR ** -0.5, 0.25, ((0, 16),)),
        "w_output": gaussian(seeds[5], (H * VD, D), (H * VD) ** -0.5, 0.046875, ((0, 16), (1, 16))),
        "latent_cache": draw_latent_cache(jax.random.fold_in(seeds[10], 71), 0),
        "context_lengths": draw_context_lengths(jax.random.fold_in(seeds[10], 71), 0),
        "block_ids": draw_block_ids(jax.random.fold_in(seeds[10], 71), 0),
        "block_counts": draw_block_counts(jax.random.fold_in(seeds[10], 71), 0),
    }


def rotate(part, positions):
    half = part.shape[-1] // 2
    freq = 10000.0 ** (-(jnp.arange(half, dtype=jnp.float32) * 2.0 / part.shape[-1]))
    angle = positions.astype(jnp.float32)[:, None] * freq[None, :]
    cosine = jnp.cos(angle)[:, None, :]
    sine = jnp.sin(angle)[:, None, :]
    first = part[..., :half]
    second = part[..., half:]
    return jnp.concatenate([first * cosine - second * sine, first * sine + second * cosine], -1)

def reference(compressed_query, query_gain, w_query, w_key, value_up_weight, w_output, latent_cache, context_lengths, block_ids, block_counts):
    source = compressed_query.astype(jnp.float32)
    normed = (source * lax.rsqrt(lax.optimization_barrier(jnp.mean(source * source, -1, keepdims=True)) + 1e-06) * query_gain).astype(jnp.bfloat16)
    query = jnp.dot(normed, w_query, preferred_element_type=jnp.float32).reshape(ROWS, H, NOPE + ROPE)
    query_nope = query[..., :NOPE].astype(jnp.bfloat16)
    query_rope = rotate(query[..., NOPE:], context_lengths - 1).astype(jnp.bfloat16)
    query_latent = jnp.einsum('rhn,hnk->rhk', query_nope.astype(jnp.float32), w_key.astype(jnp.float32)).astype(jnp.bfloat16)
    full_query = jnp.concatenate([query_latent, query_rope], -1)
    scale = (NOPE + ROPE) ** (-0.5)

    def one_row(items):
        row_query, row_cache, row_ids, row_count, row_length = items
        safe_ids = jnp.maximum(row_ids, 0).astype(jnp.int32)
        positions = (safe_ids[:, None] * BLK + jnp.arange(BLK, dtype=jnp.int32)[None, :]).reshape(-1)
        keys = row_cache[positions]
        slot_live = (jnp.arange(NSEL, dtype=jnp.int32) < row_count)[:, None]
        live = (slot_live & (positions.reshape(NSEL, BLK) < row_length)).reshape(-1)
        scores = jnp.dot(row_query, keys.T, preferred_element_type=jnp.float32) * scale
        largest = lax.optimization_barrier(jnp.max(jnp.where(live[None, :], scores, -1e+30), -1, keepdims=True))
        weights = jnp.where(live[None, :], jnp.exp(scores - largest), 0.0)
        total = lax.optimization_barrier(jnp.sum(weights, -1, keepdims=True))
        summed = jnp.dot(weights.astype(jnp.bfloat16), keys[:, :KVR], preferred_element_type=jnp.float32)
        return (summed / total).astype(jnp.bfloat16)
    attended_latent_rows = lax.map(one_row, (full_query, latent_cache, block_ids, block_counts, context_lengths))
    value_rows = jnp.einsum('sat,atl->sal', attended_latent_rows.astype(jnp.float32), value_up_weight.astype(jnp.float32)).astype(jnp.bfloat16)
    flat = value_rows.reshape(ROWS, H * VD)
    return jnp.dot(flat, w_output, preferred_element_type=jnp.float32).astype(jnp.bfloat16)
```

```python
import functools

import jax
import jax.numpy as jnp
from jax import lax
from jax.experimental import pallas as pl
from jax.experimental.pallas import tpu as pltpu
from jax.sharding import PartitionSpec as P

NOPE = 128
ROPE = 64
KVR = 512
QK = KVR + ROPE
HEAD = NOPE + ROPE
BLK = 64
SLOTS = 4
ROWS = 8
HEADS = 8
LANES = 128
MESH = pl.DeviceIdType.MESH
F32 = jnp.float32
BF16 = jnp.bfloat16


def kernel(
    n,
    lens,
    ids,
    counts,
    cq_hbm,
    gain,
    wq_hbm,
    wk_hbm,
    vup_hbm,
    wo_hbm,
    cache_hbm,
    out,
    cq,
    wq,
    wk,
    vup,
    wo,
    cache,
    keys,
    tokens_at,
    a_send,
    a_recv,
    q_rows,
    b_send,
    q_all,
    o_send,
    l_send,
    o_recv,
    l_recv,
    f_send,
    f_recv,
    f_rows,
    v_all,
    h_send,
    h_recv,
    local_sem,
    a_ss,
    a_rs,
    b_sem,
    c_ss,
    c_rs,
    e_ss,
    e_rs,
    l_ss,
    l_rs,
    f_sem,
    g_ss,
    g_rs,
    h_ss,
    h_rs,
):
    c = lax.axis_index("cache")
    p = lax.axis_index("proj")
    barrier = pltpu.get_barrier_semaphore()

    def greet(i, carry):
        pl.semaphore_signal(
            barrier, inc=1, device_id=(lax.rem(c + i, n), p), device_id_type=MESH
        )
        pl.semaphore_signal(
            barrier, inc=1, device_id=(c, lax.rem(p + i, n)), device_id_type=MESH
        )
        return carry

    lax.fori_loop(1, n, greet, 0)

    depth = wq_hbm.shape[0]
    width = cq.shape[1]
    span = wq.shape[0]
    start = jnp.minimum((c * depth) // 128 * 128, width - span)
    inside = c * depth - start
    wq[...] = jnp.zeros_like(wq)
    loads = [
        pltpu.make_async_copy(cq_hbm, cq, local_sem.at[0]),
        pltpu.make_async_copy(
            wq_hbm, wq.at[pl.ds(pl.multiple_of(inside, 32), depth)], local_sem.at[1]
        ),
        pltpu.make_async_copy(wk_hbm, wk, local_sem.at[2]),
        pltpu.make_async_copy(cache_hbm, cache, local_sem.at[3]),
        pltpu.make_async_copy(vup_hbm, vup, local_sem.at[4]),
        pltpu.make_async_copy(wo_hbm, wo, local_sem.at[5]),
    ]
    for load in loads:
        load.start()

    loads[0].wait()
    source = cq[...].astype(F32)
    norm = lax.rsqrt(jnp.mean(source * source, -1, keepdims=True) + 1e-06)
    share = pl.ds(pl.multiple_of(start, 128), span)
    tiles = [gain[pl.ds(start // LANES + t, 1), :] for t in range(span // LANES)]
    normed = (cq[:, share].astype(F32) * norm * jnp.concatenate(tiles, 1)).astype(BF16)
    loads[1].wait()
    half = a_send.shape[2]
    tile = 256
    for t in range(half // tile):
        left = jnp.dot(normed, wq[:, t * tile : (t + 1) * tile], preferred_element_type=F32)
        right = jnp.dot(
            normed, wq[:, half + t * tile : half + (t + 1) * tile], preferred_element_type=F32
        )
        both = jnp.concatenate(
            [left.reshape(n, ROWS, tile), right.reshape(n, ROWS, tile)], axis=1
        )
        a_send[:, :, t * tile : (t + 1) * tile] = both.astype(BF16)

    pl.semaphore_wait(barrier, 2 * (n - 1))

    def a_copy(i):
        d = lax.rem(c + i, n)
        return pltpu.make_async_remote_copy(
            src_ref=a_send.at[lax.rem(d + p, n)],
            dst_ref=a_recv.at[c],
            send_sem=a_ss.at[i],
            recv_sem=a_rs.at[c],
            device_id=(d, p),
            device_id_type=MESH,
        )

    def start_all(make):
        def body(i, carry):
            make(i).start()
            return carry

        lax.fori_loop(1, n, body, 0)

    def finish_sends(make):
        def body(i, carry):
            make(i).wait_send()
            return carry

        lax.fori_loop(1, n, body, 0)

    def arrived(buffer, sems, s):
        pltpu.make_async_copy(buffer.at[s], buffer.at[s], sems.at[s]).wait()

    start_all(a_copy)

    ctx_local = cache.shape[2]
    per_shard = ctx_local // BLK
    slots = ids.shape[1]
    tokens = SLOTS * BLK

    def column(ref, base):
        rows = lax.broadcasted_iota(jnp.int32, (ROWS, 1), 0)
        found = jnp.zeros((ROWS, 1), jnp.int32)
        for r in range(ROWS):
            found = jnp.where(rows == r, ref[base + r], found)
        return found

    local = ids[...] - c * per_shard
    slot = lax.broadcasted_iota(jnp.int32, (ROWS, slots), 1)
    mine = (slot < column(counts, 0)) & (local >= 0) & (local < per_shard)
    before = lax.broadcasted_iota(jnp.int32, (slots, slots), 0) < lax.broadcasted_iota(
        jnp.int32, (slots, slots), 1
    )
    order = jnp.dot(
        mine.astype(F32), before.astype(F32), preferred_element_type=F32
    )
    lane = lax.broadcasted_iota(jnp.int32, (ROWS, tokens), 1)
    picked = jnp.full((ROWS, tokens), -1, jnp.int32)
    for k in range(SLOTS):
        kept = mine & (order == float(k))
        found = jnp.sum(jnp.where(kept, local + 1, 0), -1, keepdims=True) - 1
        picked = jnp.where(lane // BLK == k, found, picked)
    at = picked * BLK + lane % BLK
    live_at = (picked >= 0) & (c * ctx_local + at < column(lens, p * ROWS))
    tokens_at[...] = jnp.where(live_at, at, -1)

    loads[3].wait()

    def gather(r, carry):
        chosen = lax.broadcasted_iota(jnp.int32, (ctx_local, tokens), 0) == tokens_at[
            pl.ds(r, 1), :
        ]
        keys[r] = jnp.dot(
            cache[r], chosen.astype(F32).astype(BF16), preferred_element_type=F32
        ).astype(BF16)
        return carry

    lax.fori_loop(0, ROWS, gather, 0)

    block = lax.rem(c + p, n)

    def add(i, total):
        s = lax.rem(c + i, n)
        arrived(a_recv, a_rs, s)
        return total + a_recv[s].astype(F32)

    query = lax.fori_loop(1, n, add, a_send[block].astype(F32))
    half_rope = ROPE // 2
    index = lax.broadcasted_iota(jnp.int32, (1, half_rope), 1)
    freq = jnp.zeros((1, half_rope), F32)
    for i in range(half_rope):
        freq = jnp.where(index == i, float(10000.0 ** (-2.0 * i / ROPE)), freq)
    angles = (column(lens, block * ROWS) - 1).astype(F32) * freq
    angles = jnp.concatenate([angles, angles], axis=0)
    cosine, sine = jnp.cos(angles), jnp.sin(angles)
    loads[2].wait()
    per_half = HEADS // 2
    blank = jnp.zeros((2 * ROWS, LANES - ROPE), F32)
    for j in range(per_half):
        base = j * HEAD
        nope = query[:, base : base + NOPE].astype(BF16)
        first = query[:, base + NOPE : base + NOPE + ROPE // 2]
        second = query[:, base + NOPE + ROPE // 2 : base + HEAD]
        turned = jnp.concatenate(
            [first * cosine - second * sine, first * sine + second * cosine, blank], axis=1
        )
        for g in range(2):
            h = g * per_half + j
            latent = jnp.dot(nope, wk[h], preferred_element_type=F32)
            place = pl.ds(h, ROWS, stride=HEADS)
            for t in range(KVR // LANES):
                q_rows[t, place, :] = latent[g * ROWS : (g + 1) * ROWS, t * LANES : (t + 1) * LANES]
            q_rows[KVR // LANES, place, :] = turned[g * ROWS : (g + 1) * ROWS]
    for t in range(KVR // LANES):
        b_send[:, t * LANES : (t + 1) * LANES] = q_rows[t].astype(BF16)
    b_send[:, KVR:] = q_rows[KVR // LANES][:, :ROPE].astype(BF16)

    def b_remote():
        return pltpu.make_async_remote_copy(
            src_ref=b_send,
            dst_ref=q_all.at[c],
            send_sem=b_sem.at[0],
            recv_sem=b_sem.at[1],
            device_id=(c, block),
            device_id_type=MESH,
        )

    @pl.when(c != 0)
    def _():
        copy = b_remote()
        copy.start()
        copy.wait_recv()

    @pl.when(c == 0)
    def _():
        q_all[c] = b_send[...]

    def c_copy(i):
        d = lax.rem(c + i, n)
        return pltpu.make_async_remote_copy(
            src_ref=q_all.at[c],
            dst_ref=q_all.at[c],
            send_sem=c_ss.at[i],
            recv_sem=c_rs.at[c],
            device_id=(d, p),
            device_id_type=MESH,
        )

    start_all(c_copy)

    def c_wait(i, carry):
        arrived(q_all, c_rs, lax.rem(c + i, n))
        return carry

    lax.fori_loop(1, n, c_wait, 0)

    scale = HEAD ** (-0.5)
    heads = n * HEADS
    eye = lax.broadcasted_iota(jnp.int32, (heads, heads), 0) == lax.broadcasted_iota(
        jnp.int32, (heads, heads), 1
    )

    def attend(r, q):
        live = tokens_at[pl.ds(r, 1), :] >= 0
        key = keys[r]
        scores = jnp.dot(q, key, preferred_element_type=F32) * scale
        largest = jnp.max(jnp.where(live, scores, -1e30), -1, keepdims=True)
        weights = jnp.where(live, jnp.exp(scores - largest), 0.0)
        total = jnp.sum(weights, -1, keepdims=True)
        summed = lax.dot_general(
            weights.astype(BF16),
            key[:KVR],
            (((1,), (1,)), ((), ())),
            preferred_element_type=F32,
        )
        some = total > 0.0
        safe = jnp.where(some, total, 1.0)
        logs = jnp.where(some, largest + jnp.log(safe), -1e30)
        l_send[pl.ds(r, 1), :] = jnp.sum(jnp.where(eye, logs, 0.0), 0, keepdims=True)
        return summed * (1.0 / safe)

    def pair(m, carry):
        two = pl.ds(pl.multiple_of(m * 16, 16), 16)
        q = q_all[:, two, :].astype(F32)
        first = attend(2 * m, q[:, :ROWS, :].reshape(heads, QK).astype(BF16))
        second = attend(2 * m + 1, q[:, ROWS:, :].reshape(heads, QK).astype(BF16))
        o_send[:, two, :] = jnp.concatenate(
            [first.reshape(n, HEADS, KVR), second.reshape(n, HEADS, KVR)], axis=1
        ).astype(BF16)
        return carry

    lax.fori_loop(0, ROWS // 2, pair, 0)

    def e_copy(i):
        d = lax.rem(c + i, n)
        return pltpu.make_async_remote_copy(
            src_ref=o_send.at[d],
            dst_ref=o_recv.at[c],
            send_sem=e_ss.at[i],
            recv_sem=e_rs.at[c],
            device_id=(d, p),
            device_id_type=MESH,
        )

    def l_copy(i):
        d = lax.rem(c + i, n)
        return pltpu.make_async_remote_copy(
            src_ref=l_send,
            dst_ref=l_recv.at[c],
            send_sem=l_ss.at[i],
            recv_sem=l_rs.at[c],
            device_id=(d, p),
            device_id_type=MESH,
        )

    start_all(l_copy)
    start_all(e_copy)
    o_recv[c] = o_send[c]
    l_recv[c] = l_send[...]

    def l_wait(i, carry):
        arrived(l_recv, l_rs, lax.rem(c + i, n))
        return carry

    lax.fori_loop(1, n, l_wait, 0)
    logs = l_recv[...]
    raised = jnp.exp(logs - jnp.max(logs, 0, keepdims=True))
    l_recv[...] = raised / jnp.sum(raised, 0, keepdims=True)
    own = ROWS * HEADS
    mask = (
        lax.broadcasted_iota(jnp.int32, (own, heads), 1)
        == c * HEADS + lax.broadcasted_iota(jnp.int32, (own, heads), 0) % HEADS
    )

    def weigh(s):
        factor = jnp.broadcast_to(l_recv[s][:, None, :], (ROWS, HEADS, heads)).reshape(own, heads)
        column = jnp.sum(jnp.where(mask, factor, 0.0), -1, keepdims=True)
        return o_recv[s].astype(F32) * column

    def combine(i, total):
        s = lax.rem(c + i, n)
        arrived(o_recv, e_rs, s)
        return total + weigh(s)

    attended = lax.fori_loop(1, n, combine, weigh(c))
    f_send[...] = attended.astype(BF16)

    def f_remote():
        return pltpu.make_async_remote_copy(
            src_ref=f_send,
            dst_ref=f_recv,
            send_sem=f_sem.at[0],
            recv_sem=f_sem.at[1],
            device_id=(c, lax.rem(p + n - c, n)),
            device_id_type=MESH,
        )

    @pl.when(c != 0)
    def _():
        copy = f_remote()
        copy.start()
        copy.wait_recv()

    @pl.when(c == 0)
    def _():
        f_recv[...] = f_send[...]

    loads[4].wait()
    for t in range(KVR // LANES):
        f_rows[t] = f_recv[:, t * LANES : (t + 1) * LANES].astype(F32)
    values = [
        jnp.dot(
            jnp.concatenate(
                [f_rows[t, pl.ds(h, ROWS, stride=HEADS), :] for t in range(KVR // LANES)], 1
            ).astype(BF16),
            vup[h],
            preferred_element_type=F32,
        )
        for h in range(HEADS)
    ]
    v_all[c] = jnp.concatenate(
        [jnp.concatenate(values[:per_half], 1), jnp.concatenate(values[per_half:], 1)], 0
    ).astype(BF16)

    def g_copy(i):
        d = lax.rem(c + i, n)
        return pltpu.make_async_remote_copy(
            src_ref=v_all.at[c],
            dst_ref=v_all.at[c],
            send_sem=g_ss.at[i],
            recv_sem=g_rs.at[c],
            device_id=(d, p),
            device_id_type=MESH,
        )

    start_all(g_copy)
    loads[5].wait()

    def g_wait(i, carry):
        arrived(v_all, g_rs, lax.rem(c + i, n))
        return carry

    lax.fori_loop(1, n, g_wait, 0)

    v = v_all[...].astype(F32)
    wide = v.shape[2]
    rows = n * ROWS
    low = v[:, :ROWS, :].reshape(rows, wide).astype(BF16)
    high = v[:, ROWS:, :].reshape(rows, wide).astype(BF16)
    across = (((1,), (1,)), ((), ()))
    result = lax.dot_general(
        low, wo[:, :wide], across, preferred_element_type=F32
    ) + lax.dot_general(high, wo[:, wide:], across, preferred_element_type=F32)
    columns = wo.shape[0]
    cut = h_send.shape[2]
    rest = jnp.concatenate(
        [result[:, cut:], jnp.zeros((rows, 2 * cut - columns), F32)], axis=1
    )
    h_send[...] = jnp.concatenate(
        [result[:, :cut].reshape(n, ROWS, cut), rest.reshape(n, ROWS, cut)], axis=1
    ).astype(BF16)

    def h_copy(i):
        return pltpu.make_async_remote_copy(
            src_ref=h_send.at[i],
            dst_ref=h_recv.at[p],
            send_sem=h_ss.at[i],
            recv_sem=h_rs.at[p],
            device_id=(c, lax.rem(p + i, n)),
            device_id_type=MESH,
        )

    start_all(h_copy)

    def h_add(i, total):
        s = lax.rem(p + i, n)
        arrived(h_recv, h_rs, s)
        return total + h_recv[s].astype(F32)

    summed = lax.fori_loop(1, n, h_add, h_send[0].astype(F32))
    out[...] = jnp.concatenate(
        [summed[:ROWS], summed[ROWS:, : columns - cut]], axis=1
    ).astype(BF16)

    for make in (a_copy, c_copy, e_copy, l_copy, g_copy, h_copy):
        finish_sends(make)

    @pl.when(c != 0)
    def _():
        b_remote().wait_send()
        f_remote().wait_send()


def on_device(
    compressed_query,
    query_gain,
    w_query,
    w_key,
    value_up_weight,
    w_output,
    latent_cache,
    context_lengths,
    block_ids,
    block_counts,
):
    n = lax.axis_size("cache")
    rows, rank = compressed_query.shape
    depth, columns = w_query.shape
    span = 256
    w_output = w_output.T
    latent_cache = latent_cache.transpose(0, 2, 1)
    heads = n * HEADS
    own = ROWS * HEADS
    out_columns = w_output.shape[0]
    smem = pl.BlockSpec(memory_space=pltpu.SMEM)
    vmem = pl.BlockSpec(memory_space=pltpu.VMEM)
    hbm = pl.BlockSpec(memory_space=pl.ANY)
    many = pltpu.SemaphoreType.DMA((n,))
    two = pltpu.SemaphoreType.DMA((2,))
    return pl.pallas_call(
        functools.partial(kernel, n),
        out_shape=jax.ShapeDtypeStruct((ROWS, out_columns), BF16),
        in_specs=[smem, vmem, smem, hbm, vmem, hbm, hbm, hbm, hbm, hbm],
        out_specs=vmem,
        scratch_shapes=[
            pltpu.VMEM((rows, rank), BF16),
            pltpu.VMEM((span, columns), BF16),
            pltpu.VMEM(w_key.shape, BF16),
            pltpu.VMEM(value_up_weight.shape, BF16),
            pltpu.VMEM(w_output.shape, BF16),
            pltpu.VMEM(latent_cache.shape, BF16),
            pltpu.VMEM((ROWS, QK, SLOTS * BLK), BF16),
            pltpu.VMEM((ROWS, SLOTS * BLK), jnp.int32),
            pltpu.VMEM((n, 2 * ROWS, columns // 2), BF16),
            pltpu.VMEM((n, 2 * ROWS, columns // 2), BF16),
            pltpu.VMEM((KVR // LANES + 1, own, LANES), F32),
            pltpu.VMEM((own, QK), BF16),
            pltpu.VMEM((n, own, QK), BF16),
            pltpu.VMEM((n, own, KVR), BF16),
            pltpu.VMEM((ROWS, heads), F32),
            pltpu.VMEM((n, own, KVR), BF16),
            pltpu.VMEM((n, ROWS, heads), F32),
            pltpu.VMEM((own, KVR), BF16),
            pltpu.VMEM((own, KVR), BF16),
            pltpu.VMEM((KVR // LANES, own, LANES), F32),
            pltpu.VMEM((n, 2 * ROWS, HEADS // 2 * NOPE), BF16),
            pltpu.VMEM((n, 2 * ROWS, 256), BF16),
            pltpu.VMEM((n, 2 * ROWS, 256), BF16),
            pltpu.SemaphoreType.DMA((6,)),
            many,
            many,
            two,
            many,
            many,
            many,
            many,
            many,
            many,
            two,
            many,
            many,
            many,
            many,
        ],
        compiler_params=pltpu.CompilerParams(
            collective_id=0, has_side_effects=True, vmem_limit_bytes=56 * 2**20
        ),
    )(
        context_lengths,
        block_ids,
        block_counts,
        compressed_query,
        query_gain.reshape(rank // LANES, LANES),
        w_query,
        w_key,
        value_up_weight,
        w_output,
        latent_cache,
    )


def solution(mesh):
    placed = (
        P(),
        P(),
        P("cache", "proj"),
        P("proj", None, None),
        P("proj", None, None),
        P("proj", "cache"),
        P("proj", "cache", None),
        P(),
        P("proj", None),
        P("proj"),
    )
    return jax.shard_map(
        on_device, mesh=mesh, in_specs=placed, out_specs=P("proj", "cache"), check_vma=False
    )
```

```python
import functools

import jax
import jax.numpy as jnp
from jax import lax
from jax.experimental import pallas as pl
from jax.experimental.pallas import tpu as pltpu
from jax.sharding import PartitionSpec as P

NOPE = 128
ROPE = 64
KVR = 512
QK = KVR + ROPE
HEAD = NOPE + ROPE
BLK = 64
SLOTS = 4
ROWS = 8
HEADS = 8
LANES = 128
SIDE = 4
RING = (1, 3, 2)
FAR_FIRST = sorted(
    [(i, j) for i in range(SIDE) for j in range(SIDE) if i or j],
    key=lambda at: -min(at[0], SIDE - at[0]) - min(at[1], SIDE - at[1]),
)
MESH = pl.DeviceIdType.MESH
F32 = jnp.float32
BF16 = jnp.bfloat16


def kernel(
    n,
    lens,
    ids,
    counts,
    cq_hbm,
    gain,
    wq_hbm,
    wk_hbm,
    vup_hbm,
    wo_hbm,
    cache_hbm,
    out,
    cq,
    wq,
    wk,
    vup,
    wo,
    cache,
    keys,
    tokens_at,
    a_send,
    a_recv,
    q_rows,
    b_send,
    q_all,
    o_send,
    o_first,
    o_merged,
    o_second,
    l_send,
    l_first,
    l_ratio,
    l_next,
    l_second,
    f_send,
    f_recv,
    f_rows,
    v_all,
    h_send,
    h_recv,
    local_sem,
    a_ss,
    a_rs,
    b_ss,
    b_rs,
    c_ss,
    c_rs,
    e_ss,
    e_rs,
    e2_ss,
    e2_rs,
    l_ss,
    l_rs,
    f_sem,
    g_ss,
    g_rs,
    h_ss,
    h_rs,
):
    c = lax.axis_index("cache")
    p = lax.axis_index("proj")
    x, y = c // SIDE, lax.rem(c, SIDE)

    def on_x(i):
        return lax.rem(x + i, SIDE) * SIDE + y

    def on_y(i):
        return x * SIDE + lax.rem(y + i, SIDE)

    def on_plane(k):
        dx, dy = FAR_FIRST[k]
        return lax.rem(x + dx, SIDE) * SIDE + lax.rem(y + dy, SIDE)

    def send(src, dst, send_sem, recv_sem, cache_at, proj_at):
        return pltpu.make_async_remote_copy(
            src_ref=src,
            dst_ref=dst,
            send_sem=send_sem,
            recv_sem=recv_sem,
            device_id=(cache_at, proj_at),
            device_id_type=MESH,
        )

    def arrived(ref, sem):
        pltpu.make_async_copy(ref, ref, sem).wait()

    sent = []

    def go(*copy):
        copy = send(*copy)
        copy.start()
        sent.append(copy)

    barrier = pltpu.get_barrier_semaphore()

    def greet(i, carry):
        pl.semaphore_signal(
            barrier, inc=1, device_id=(lax.rem(c + i, n), p), device_id_type=MESH
        )
        pl.semaphore_signal(
            barrier, inc=1, device_id=(c, lax.rem(p + i, n)), device_id_type=MESH
        )
        return carry

    lax.fori_loop(1, n, greet, 0)

    depth = wq_hbm.shape[0]
    width = cq.shape[1]
    span = wq.shape[0]
    start = jnp.minimum((c * depth) // 128 * 128, width - span)
    inside = c * depth - start
    wq[...] = jnp.zeros_like(wq)
    loads = [
        pltpu.make_async_copy(cq_hbm, cq, local_sem.at[0]),
        pltpu.make_async_copy(
            wq_hbm, wq.at[pl.ds(pl.multiple_of(inside, 32), depth)], local_sem.at[1]
        ),
        pltpu.make_async_copy(wk_hbm, wk, local_sem.at[2]),
        pltpu.make_async_copy(cache_hbm, cache, local_sem.at[3]),
        pltpu.make_async_copy(vup_hbm, vup, local_sem.at[4]),
        pltpu.make_async_copy(wo_hbm, wo, local_sem.at[5]),
    ]
    for load in loads:
        load.start()

    loads[0].wait()
    source = cq[...].astype(F32)
    norm = lax.rsqrt(jnp.mean(source * source, -1, keepdims=True) + 1e-06)
    share = pl.ds(pl.multiple_of(start, 128), span)
    tiles = [gain[pl.ds(start // LANES + t, 1), :] for t in range(span // LANES)]
    normed = (cq[:, share].astype(F32) * norm * jnp.concatenate(tiles, 1)).astype(BF16)
    loads[1].wait()
    half = a_send.shape[2]
    tile = 256
    for t in range(half // tile):
        left = jnp.dot(normed, wq[:, t * tile : (t + 1) * tile], preferred_element_type=F32)
        right = jnp.dot(
            normed, wq[:, half + t * tile : half + (t + 1) * tile], preferred_element_type=F32
        )
        both = jnp.concatenate(
            [left.reshape(n, ROWS, tile), right.reshape(n, ROWS, tile)], axis=1
        )
        a_send[:, :, t * tile : (t + 1) * tile] = both.astype(BF16)

    pl.semaphore_wait(barrier, 2 * (n - 1))

    for k in range(n - 1):
        d = on_plane(k)
        go(a_send.at[lax.rem(d + p, n)], a_recv.at[c], a_ss.at[k], a_rs.at[c], d, p)

    ctx_local = cache.shape[2]
    per_shard = ctx_local // BLK
    slots = ids.shape[1]
    tokens = SLOTS * BLK

    def column(ref, base):
        rows = lax.broadcasted_iota(jnp.int32, (ROWS, 1), 0)
        found = jnp.zeros((ROWS, 1), jnp.int32)
        for r in range(ROWS):
            found = jnp.where(rows == r, ref[base + r], found)
        return found

    local = ids[...] - c * per_shard
    slot = lax.broadcasted_iota(jnp.int32, (ROWS, slots), 1)
    mine = (slot < column(counts, 0)) & (local >= 0) & (local < per_shard)
    before = lax.broadcasted_iota(jnp.int32, (slots, slots), 0) < lax.broadcasted_iota(
        jnp.int32, (slots, slots), 1
    )
    order = jnp.dot(
        mine.astype(F32), before.astype(F32), preferred_element_type=F32
    )
    lane = lax.broadcasted_iota(jnp.int32, (ROWS, tokens), 1)
    picked = jnp.full((ROWS, tokens), -1, jnp.int32)
    for k in range(SLOTS):
        kept = mine & (order == float(k))
        found = jnp.sum(jnp.where(kept, local + 1, 0), -1, keepdims=True) - 1
        picked = jnp.where(lane // BLK == k, found, picked)
    at = picked * BLK + lane % BLK
    live_at = (picked >= 0) & (c * ctx_local + at < column(lens, p * ROWS))
    tokens_at[...] = jnp.where(live_at, at, -1)

    loads[3].wait()

    def gather(r, carry):
        chosen = lax.broadcasted_iota(jnp.int32, (ctx_local, tokens), 0) == tokens_at[
            pl.ds(r, 1), :
        ]
        keys[r] = jnp.dot(
            cache[r], chosen.astype(F32).astype(BF16), preferred_element_type=F32
        ).astype(BF16)
        return carry

    lax.fori_loop(0, ROWS, gather, 0)

    block = lax.rem(c + p, n)

    def add(i, total):
        s = lax.rem(c + i, n)
        arrived(a_recv.at[s], a_rs.at[s])
        return total + a_recv[s].astype(F32)

    query = lax.fori_loop(1, n, add, a_send[block].astype(F32))
    half_rope = ROPE // 2
    index = lax.broadcasted_iota(jnp.int32, (1, half_rope), 1)
    freq = jnp.zeros((1, half_rope), F32)
    for i in range(half_rope):
        freq = jnp.where(index == i, float(10000.0 ** (-2.0 * i / ROPE)), freq)
    angles = (column(lens, block * ROWS) - 1).astype(F32) * freq
    angles = jnp.concatenate([angles, angles], axis=0)
    cosine, sine = jnp.cos(angles), jnp.sin(angles)
    loads[2].wait()
    per_half = HEADS // 2
    blank = jnp.zeros((2 * ROWS, LANES - ROPE), F32)
    for j in range(per_half):
        base = j * HEAD
        nope = query[:, base : base + NOPE].astype(BF16)
        first = query[:, base + NOPE : base + NOPE + ROPE // 2]
        second = query[:, base + NOPE + ROPE // 2 : base + HEAD]
        turned = jnp.concatenate(
            [first * cosine - second * sine, first * sine + second * cosine, blank], axis=1
        )
        for g in range(2):
            h = g * per_half + j
            latent = jnp.dot(nope, wk[h], preferred_element_type=F32)
            place = pl.ds(h, ROWS, stride=HEADS)
            for t in range(KVR // LANES):
                q_rows[t, place, :] = latent[g * ROWS : (g + 1) * ROWS, t * LANES : (t + 1) * LANES]
            q_rows[KVR // LANES, place, :] = turned[g * ROWS : (g + 1) * ROWS]
    own = ROWS * HEADS
    part = own // 2
    latent_tiles = KVR // LANES
    for g in range(2):
        for t in range(latent_tiles):
            b_send[g, t * part : (t + 1) * part, :] = q_rows[
                t, g * part : (g + 1) * part, :
            ].astype(BF16)
        low = q_rows[latent_tiles, g * part : g * part + part // 2, :]
        high = q_rows[latent_tiles, g * part + part // 2 : (g + 1) * part, :]
        b_send[g, latent_tiles * part :, :] = jnp.concatenate(
            [low[:, :ROPE], high[:, :ROPE]], axis=1
        ).astype(BF16)

    def b_copy(g):
        return send(b_send.at[g], q_all.at[c, g], b_ss.at[g], b_rs.at[g], c, block)

    @pl.when(c != 0)
    def _():
        b_copy(0).start()
        b_copy(1).start()

    @pl.when(c == 0)
    def _():
        q_all[c] = b_send[...]

    count = iter(range(30))

    def spread(s, g, to):
        k = next(count)
        go(q_all.at[s, g], q_all.at[s, g], c_ss.at[k], c_rs.at[s, g], to, p)

    def got(s, g):
        arrived(q_all.at[s, g], c_rs.at[s, g])

    @pl.when(c != 0)
    def _():
        b_copy(0).wait_recv()

    for i in RING:
        spread(c, 0, on_x(i))

    @pl.when(c != 0)
    def _():
        b_copy(1).wait_recv()

    for i in RING:
        spread(c, 1, on_y(i))
    for i in RING:
        spread(c, 0, on_y(i))
        spread(c, 1, on_x(i))
    for i in RING:
        s = on_x(i)
        got(s, 0)
        for j in RING:
            spread(s, 0, on_y(j))
        s = on_y(i)
        got(s, 1)
        for j in RING:
            spread(s, 1, on_x(j))
    for i in RING:
        got(on_y(i), 0)
        got(on_x(i), 1)
    for dx, dy in FAR_FIRST:
        if dx and dy:
            s = lax.rem(x + dx, SIDE) * SIDE + lax.rem(y + dy, SIDE)
            got(s, 0)
            got(s, 1)

    scale = HEAD ** (-0.5)
    heads = n * HEADS
    eye = lax.broadcasted_iota(jnp.int32, (heads, heads), 0) == lax.broadcasted_iota(
        jnp.int32, (heads, heads), 1
    )

    half_count = ROWS // 2

    def attend(r, q):
        live = tokens_at[r : r + 1, :] >= 0
        key = keys[r]
        scores = jnp.dot(q, key, preferred_element_type=F32) * scale
        largest = jnp.max(jnp.where(live, scores, -1e30), -1, keepdims=True)
        weights = jnp.where(live, jnp.exp(scores - largest), 0.0)
        total = jnp.sum(weights, -1, keepdims=True)
        summed = lax.dot_general(
            weights.astype(BF16),
            key[:KVR],
            (((1,), (1,)), ((), ())),
            preferred_element_type=F32,
        )
        some = total > 0.0
        safe = jnp.where(some, total, 1.0)
        logs = jnp.where(some, largest + jnp.log(safe), -1e30)
        l_send[r // half_count, r % half_count : r % half_count + 1, :] = jnp.sum(jnp.where(eye, logs, 0.0), 0, keepdims=True)
        return summed * (1.0 / safe)

    def pair(m):
        g, j = m // 2, m % 2
        tiles = [
            q_all[:, g, t * part + j * 16 : t * part + j * 16 + 16, :] for t in range(latent_tiles)
        ]
        tiles.append(q_all[:, g, latent_tiles * part :, j * ROPE : (j + 1) * ROPE])
        q = jnp.concatenate([tile.astype(F32) for tile in tiles], axis=2)
        first = attend(2 * m, q[:, :ROWS, :].reshape(heads, QK).astype(BF16))
        second = attend(2 * m + 1, q[:, ROWS:, :].reshape(heads, QK).astype(BF16))
        both = jnp.concatenate(
            [first.reshape(n, HEADS, KVR), second.reshape(n, HEADS, KVR)], axis=1
        ).astype(BF16)
        o_send[:, :, m * 16 : (m + 1) * 16, :] = both.reshape(SIDE, SIDE, 16, KVR)

    def rows_of(g):
        return pl.ds(g * part, part)

    def piece(g, first, second):
        here = (first, second) if g == 0 else (second, first)
        return o_send.at[here[0], here[1], rows_of(g), :]

    mine = (x, y)
    along = (on_x, on_y)
    count_1 = iter(range(24))
    count_l = iter(range(12))

    def first_stage(g):
        for i in RING:
            k = next(count_l)
            go(l_send.at[g], l_first.at[g, mine[g]], l_ss.at[k], l_rs.at[g, 0, mine[g]], along[g](i), p)
        for j in RING + (0,):
            to = lax.rem(mine[1 - g] + j, SIDE)
            for i in RING:
                k = next(count_1)
                at = lax.rem(mine[g] + i, SIDE)
                go(
                    piece(g, at, to),
                    o_first.at[g, mine[g], to],
                    e_ss.at[k],
                    e_rs.at[g, mine[g], to],
                    along[g](i),
                    p,
                )

    for m in range(2):
        pair(m)
    first_stage(0)
    for m in range(2, 4):
        pair(m)
    first_stage(1)

    def shares(logs):
        top = jnp.max(logs, 0, keepdims=True)
        raised = jnp.exp(logs - top)
        total = jnp.sum(raised, 0, keepdims=True)
        return raised / total, (top + jnp.log(total))[0]

    spot = lax.broadcasted_iota(jnp.int32, (part, heads), 1) - (
        lax.broadcasted_iota(jnp.int32, (part, heads), 0) % HEADS
    )

    def scaled(value, share, d):
        wide = jnp.broadcast_to(share[:, None, :], (half_count, HEADS, heads))
        wide = wide.reshape(part, heads)
        column = jnp.sum(jnp.where(spot == d * HEADS, wide, 0.0), -1, keepdims=True)
        return value.astype(F32) * column

    def slot_of(v, i):
        return lax.rem(v + i, SIDE)

    count_2 = iter(range(6))

    def weights_of(buffer, g, stage, me):
        for i in RING:
            s = slot_of(me, i)
            arrived(buffer.at[g, s], l_rs.at[g, stage, s])
        return shares(buffer[g])

    for g in range(2):
        l_first[g, mine[g]] = l_send[g]
    for g in range(2):
        share, merged = weights_of(l_first, g, 0, mine[g])
        l_ratio[g] = share
        l_next[g] = merged
        for i in RING:
            k = next(count_l)
            go(
                l_next.at[g],
                l_second.at[g, mine[1 - g]],
                l_ss.at[k],
                l_rs.at[g, 1, mine[1 - g]],
                along[1 - g](i),
                p,
            )
        l_second[g, mine[1 - g]] = merged

    def merge(g, to):
        at = (mine[0], to) if g == 0 else (to, mine[1])
        d = at[0] * SIDE + at[1]
        total = scaled(
            o_send[at[0], at[1], g * part : (g + 1) * part, :], l_ratio[g, mine[g]], d
        )
        for i in RING:
            s = slot_of(mine[g], i)
            arrived(o_first.at[g, s, to], e_rs.at[g, s, to])
            total = total + scaled(o_first[g, s, to], l_ratio[g, s], d)
        return total

    for j in RING:
        for g in range(2):
            to = slot_of(mine[1 - g], j)
            o_merged[g, to] = merge(g, to).astype(BF16)
            k = next(count_2)
            go(
                o_merged.at[g, to],
                o_second.at[g, mine[1 - g]],
                e2_ss.at[k],
                e2_rs.at[g, mine[1 - g]],
                along[1 - g](j),
                p,
            )
    kept = [merge(g, mine[1 - g]) for g in range(2)]
    for g in range(2):
        share, _ = weights_of(l_second, g, 1, mine[1 - g])
        l_ratio[g] = share
        total = scaled(kept[g], l_ratio[g, mine[1 - g]], c)
        for i in RING:
            s = slot_of(mine[1 - g], i)
            arrived(o_second.at[g, s], e2_rs.at[g, s])
            total = total + scaled(o_second[g, s], l_ratio[g, s], c)
        f_send[g * part : (g + 1) * part, :] = total.astype(BF16)

    def f_copy():
        return send(f_send, f_recv, f_sem.at[0], f_sem.at[1], c, lax.rem(p + n - c, n))

    @pl.when(c != 0)
    def _():
        f_copy().start()
        f_copy().wait_recv()

    @pl.when(c == 0)
    def _():
        f_recv[...] = f_send[...]

    loads[4].wait()
    for t in range(KVR // LANES):
        f_rows[t] = f_recv[:, t * LANES : (t + 1) * LANES].astype(F32)
    values = [
        jnp.dot(
            jnp.concatenate(
                [f_rows[t, pl.ds(h, ROWS, stride=HEADS), :] for t in range(KVR // LANES)], 1
            ).astype(BF16),
            vup[h],
            preferred_element_type=F32,
        )
        for h in range(HEADS)
    ]
    v_all[c] = jnp.concatenate(
        [jnp.concatenate(values[:per_half], 1), jnp.concatenate(values[per_half:], 1)], 0
    ).astype(BF16)

    for k in range(n - 1):
        go(v_all.at[c], v_all.at[c], g_ss.at[k], g_rs.at[c], on_plane(k), p)
    loads[5].wait()
    for k in reversed(range(n - 1)):
        d = on_plane(k)
        arrived(v_all.at[d], g_rs.at[d])

    v = v_all[...].astype(F32)
    wide = v.shape[2]
    rows = n * ROWS
    low = v[:, :ROWS, :].reshape(rows, wide).astype(BF16)
    high = v[:, ROWS:, :].reshape(rows, wide).astype(BF16)
    across = (((1,), (1,)), ((), ()))
    result = lax.dot_general(
        low, wo[:, :wide], across, preferred_element_type=F32
    ) + lax.dot_general(high, wo[:, wide:], across, preferred_element_type=F32)
    columns = wo.shape[0]
    cut = h_send.shape[2]
    rest = jnp.concatenate(
        [result[:, cut:], jnp.zeros((rows, 2 * cut - columns), F32)], axis=1
    )
    h_send[...] = jnp.concatenate(
        [result[:, :cut].reshape(n, ROWS, cut), rest.reshape(n, ROWS, cut)], axis=1
    ).astype(BF16)

    for k in range(n - 1):
        i = n // 2 + (k + 1) // 2 * (1 if k % 2 else -1)
        d = lax.rem(p + i, n)
        go(h_send.at[i], h_recv.at[p], h_ss.at[i], h_rs.at[p], c, d)

    def h_add(i, total):
        s = lax.rem(p + i, n)
        arrived(h_recv.at[s], h_rs.at[s])
        return total + h_recv[s].astype(F32)

    summed = lax.fori_loop(1, n, h_add, h_send[0].astype(F32))
    out[...] = jnp.concatenate(
        [summed[:ROWS], summed[ROWS:, : columns - cut]], axis=1
    ).astype(BF16)

    for copy in sent:
        copy.wait_send()

    @pl.when(c != 0)
    def _():
        b_copy(0).wait_send()
        b_copy(1).wait_send()
        f_copy().wait_send()


def on_device(
    compressed_query,
    query_gain,
    w_query,
    w_key,
    value_up_weight,
    w_output,
    latent_cache,
    context_lengths,
    block_ids,
    block_counts,
):
    n = lax.axis_size("cache")
    rows, rank = compressed_query.shape
    depth, columns = w_query.shape
    span = 256
    w_output = w_output.T
    latent_cache = latent_cache.transpose(0, 2, 1)
    heads = n * HEADS
    own = ROWS * HEADS
    out_columns = w_output.shape[0]
    smem = pl.BlockSpec(memory_space=pltpu.SMEM)
    vmem = pl.BlockSpec(memory_space=pltpu.VMEM)
    hbm = pl.BlockSpec(memory_space=pl.ANY)
    dma = pltpu.SemaphoreType.DMA
    half_rows = own // 2 * (KVR // LANES) + own // 4
    return pl.pallas_call(
        functools.partial(kernel, n),
        out_shape=jax.ShapeDtypeStruct((ROWS, out_columns), BF16),
        in_specs=[smem, vmem, smem, hbm, vmem, hbm, hbm, hbm, hbm, hbm],
        out_specs=vmem,
        scratch_shapes=[
            pltpu.VMEM((rows, rank), BF16),
            pltpu.VMEM((span, columns), BF16),
            pltpu.VMEM(w_key.shape, BF16),
            pltpu.VMEM(value_up_weight.shape, BF16),
            pltpu.VMEM(w_output.shape, BF16),
            pltpu.VMEM(latent_cache.shape, BF16),
            pltpu.VMEM((ROWS, QK, SLOTS * BLK), BF16),
            pltpu.VMEM((ROWS, SLOTS * BLK), jnp.int32),
            pltpu.VMEM((n, 2 * ROWS, columns // 2), BF16),
            pltpu.VMEM((n, 2 * ROWS, columns // 2), BF16),
            pltpu.VMEM((KVR // LANES + 1, own, LANES), F32),
            pltpu.VMEM((2, half_rows, LANES), BF16),
            pltpu.VMEM((n, 2, half_rows, LANES), BF16),
            pltpu.VMEM((SIDE, SIDE, own, KVR), BF16),
            pltpu.VMEM((2, SIDE, SIDE, own // 2, KVR), BF16),
            pltpu.VMEM((2, SIDE, own // 2, KVR), BF16),
            pltpu.VMEM((2, SIDE, own // 2, KVR), BF16),
            pltpu.VMEM((2, ROWS // 2, heads), F32),
            pltpu.VMEM((2, SIDE, ROWS // 2, heads), F32),
            pltpu.VMEM((2, SIDE, ROWS // 2, heads), F32),
            pltpu.VMEM((2, ROWS // 2, heads), F32),
            pltpu.VMEM((2, SIDE, ROWS // 2, heads), F32),
            pltpu.VMEM((own, KVR), BF16),
            pltpu.VMEM((own, KVR), BF16),
            pltpu.VMEM((KVR // LANES, own, LANES), F32),
            pltpu.VMEM((n, 2 * ROWS, HEADS // 2 * NOPE), BF16),
            pltpu.VMEM((n, 2 * ROWS, 256), BF16),
            pltpu.VMEM((n, 2 * ROWS, 256), BF16),
            dma((6,)),
            dma((n,)),
            dma((n,)),
            dma((2,)),
            dma((2,)),
            dma((30,)),
            dma((n, 2)),
            dma((24,)),
            dma((2, SIDE, SIDE)),
            dma((6,)),
            dma((2, SIDE)),
            dma((12,)),
            dma((2, 2, SIDE)),
            dma((2,)),
            dma((n,)),
            dma((n,)),
            dma((n,)),
            dma((n,)),
        ],
        compiler_params=pltpu.CompilerParams(
            collective_id=0, has_side_effects=True, vmem_limit_bytes=56 * 2**20
        ),
    )(
        context_lengths,
        block_ids,
        block_counts,
        compressed_query,
        query_gain.reshape(rank // LANES, LANES),
        w_query,
        w_key,
        value_up_weight,
        w_output,
        latent_cache,
    )


def solution(mesh):
    placed = (
        P(),
        P(),
        P("cache", "proj"),
        P("proj", None, None),
        P("proj", None, None),
        P("proj", "cache"),
        P("proj", "cache", None),
        P(),
        P("proj", None),
        P("proj"),
    )
    return jax.shard_map(
        on_device, mesh=mesh, in_specs=placed, out_specs=P("proj", "cache"), check_vma=False
    )
```

```python
import functools

import jax
import jax.numpy as jnp
from jax import lax
from jax.experimental import pallas as pl
from jax.experimental.pallas import tpu as pltpu
from jax.sharding import PartitionSpec as P

NOPE = 128
ROPE = 64
KVR = 512
QK = KVR + ROPE
HEAD = NOPE + ROPE
BLK = 64
SLOTS = 4
ROWS = 8
HEADS = 8
LANES = 128
SIDE = 4
RING = (1, 3, 2)
FAR_FIRST = sorted(
    [(i, j) for i in range(SIDE) for j in range(SIDE) if i or j],
    key=lambda at: -min(at[0], SIDE - at[0]) - min(at[1], SIDE - at[1]),
)
MESH = pl.DeviceIdType.MESH
F32 = jnp.float32
BF16 = jnp.bfloat16


def kernel(
    n,
    lens,
    ids,
    counts,
    cq_hbm,
    gain,
    wq_hbm,
    wk_hbm,
    vup_hbm,
    wo_hbm,
    cache_hbm,
    out,
    cq,
    wq,
    wk,
    vup,
    wo,
    cache,
    keys,
    tokens_at,
    a_pair,
    a_send,
    a_recv,
    q_rows,
    b_send,
    q_all,
    o_send,
    o_first,
    o_merged,
    o_second,
    o_kept,
    l_send,
    l_first,
    l_first_share,
    l_second_share,
    l_next,
    l_second,
    f_send,
    f_recv,
    f_rows,
    v_all,
    h_send,
    h_recv,
    local_sem,
    a_ss,
    a_rs,
    b_ss,
    b_rs,
    c_ss,
    c_rs,
    e_ss,
    e_rs,
    l_ss,
    l_rs,
    f_ss,
    f_rs,
    g_sem,
    h_sem,
):
    c = lax.axis_index("cache")
    p = lax.axis_index("proj")
    x, y = c // SIDE, lax.rem(c, SIDE)

    def on_x(i):
        return lax.rem(x + i, SIDE) * SIDE + y

    def on_y(i):
        return x * SIDE + lax.rem(y + i, SIDE)

    def on_plane(k):
        dx, dy = FAR_FIRST[k]
        return lax.rem(x + dx, SIDE) * SIDE + lax.rem(y + dy, SIDE)

    def send(src, dst, send_sem, recv_sem, cache_at, proj_at):
        return pltpu.make_async_remote_copy(
            src_ref=src,
            dst_ref=dst,
            send_sem=send_sem,
            recv_sem=recv_sem,
            device_id=(cache_at, proj_at),
            device_id_type=MESH,
        )

    def arrived(ref, sem):
        pltpu.make_async_copy(ref, ref, sem).wait()

    def go(*copy):
        send(*copy).start()

    barrier = pltpu.get_barrier_semaphore()

    def greet(i, carry):
        pl.semaphore_signal(
            barrier, inc=1, device_id=(lax.rem(c + i, n), p), device_id_type=MESH
        )
        pl.semaphore_signal(
            barrier, inc=1, device_id=(c, lax.rem(p + i, n)), device_id_type=MESH
        )
        return carry

    lax.fori_loop(1, n, greet, 0)

    depth = wq_hbm.shape[0]
    width = cq.shape[1]
    span = wq.shape[0]
    start = jnp.minimum((c * depth) // 128 * 128, width - span)
    inside = c * depth - start
    wq[...] = jnp.zeros_like(wq)
    loads = [
        pltpu.make_async_copy(cq_hbm, cq, local_sem.at[0]),
        pltpu.make_async_copy(
            wq_hbm, wq.at[pl.ds(pl.multiple_of(inside, 32), depth)], local_sem.at[1]
        ),
        pltpu.make_async_copy(wk_hbm, wk, local_sem.at[2]),
        pltpu.make_async_copy(cache_hbm, cache, local_sem.at[3]),
        pltpu.make_async_copy(vup_hbm, vup, local_sem.at[4]),
        pltpu.make_async_copy(wo_hbm, wo, local_sem.at[5]),
    ]
    for load in loads:
        load.start()

    loads[0].wait()
    source = cq[...].astype(F32)
    norm = lax.rsqrt(jnp.mean(source * source, -1, keepdims=True) + 1e-06)
    share = pl.ds(pl.multiple_of(start, 128), span)
    tiles = [gain[pl.ds(start // LANES + t, 1), :] for t in range(span // LANES)]
    normed = (cq[:, share].astype(F32) * norm * jnp.concatenate(tiles, 1)).astype(BF16)
    loads[1].wait()
    turned_rows = pltpu.roll(normed.astype(F32).reshape(n, ROWS, span), ROWS // 2, 1)
    turned_rows = turned_rows.reshape(normed.shape).astype(BF16)
    quarter = a_send.shape[3]
    upper = lax.broadcasted_iota(jnp.int32, (n, ROWS, quarter), 1) < ROWS // 2
    for k in range(2):
        even = jnp.dot(
            normed, wq[:, 2 * k * quarter : (2 * k + 1) * quarter], preferred_element_type=F32
        ).reshape(n, ROWS, quarter)
        odd = jnp.dot(
            turned_rows,
            wq[:, (2 * k + 1) * quarter : (2 * k + 2) * quarter],
            preferred_element_type=F32,
        ).reshape(n, ROWS, quarter)
        a_pair[0, k] = jnp.where(upper, even, odd)
        a_pair[1, k] = jnp.where(upper, odd, even)
    for w in range(2):
        a_send[w] = jnp.concatenate([a_pair[w, 0], a_pair[w, 1]], axis=1).astype(BF16)

    pl.semaphore_wait(barrier, 2 * (n - 1))

    for w in range(2):
        for k in range(n - 1):
            d = on_plane(k)
            go(
                a_send.at[w, lax.rem(d + n - p, n)], a_recv.at[w, c], a_ss.at[w], a_rs.at[w], d, p
            )

    ctx_local = cache.shape[2]
    per_shard = ctx_local // BLK
    slots = ids.shape[1]
    tokens = SLOTS * BLK

    def column(ref, base, count=ROWS, repeats=1):
        rows = lax.broadcasted_iota(jnp.int32, (count * repeats, 1), 0)
        found = jnp.zeros((count * repeats, 1), jnp.int32)
        for r in range(count):
            found = jnp.where(rows % count == r, ref[base + r], found)
        return found

    local = ids[...] - c * per_shard
    slot = lax.broadcasted_iota(jnp.int32, (ROWS, slots), 1)
    mine = (slot < column(counts, 0)) & (local >= 0) & (local < per_shard)
    before = lax.broadcasted_iota(jnp.int32, (slots, slots), 0) < lax.broadcasted_iota(
        jnp.int32, (slots, slots), 1
    )
    order = jnp.dot(
        mine.astype(F32), before.astype(F32), preferred_element_type=F32
    )
    lane = lax.broadcasted_iota(jnp.int32, (ROWS, tokens), 1)
    picked = jnp.full((ROWS, tokens), -1, jnp.int32)
    for k in range(SLOTS):
        kept = mine & (order == float(k))
        found = jnp.sum(jnp.where(kept, local + 1, 0), -1, keepdims=True) - 1
        picked = jnp.where(lane // BLK == k, found, picked)
    at = picked * BLK + lane % BLK
    live_at = (picked >= 0) & (c * ctx_local + at < column(lens, p * ROWS))
    tokens_at[...] = jnp.where(live_at, at, -1)

    loads[3].wait()

    def gather(r, carry):
        chosen = lax.broadcasted_iota(jnp.int32, (ctx_local, tokens), 0) == tokens_at[
            pl.ds(r, 1), :
        ]
        keys[r] = jnp.dot(
            cache[r], chosen.astype(F32).astype(BF16), preferred_element_type=F32
        ).astype(BF16)
        return carry

    lax.fori_loop(0, ROWS, gather, 0)

    block = lax.rem(c + n - p, n)
    home = block == p

    others = pl.ds(0, n - 1)
    half_rope = ROPE // 2
    index = lax.broadcasted_iota(jnp.int32, (1, half_rope), 1)
    freq = jnp.zeros((1, half_rope), F32)
    for i in range(half_rope):
        freq = jnp.where(index == i, float(10000.0 ** (-2.0 * i / ROPE)), freq)
    four = ROWS // 2
    cosine, sine = [], []
    for w in range(2):
        angles = (column(lens, block * ROWS + w * four, four, 4) - 1).astype(F32) * freq
        cosine.append(jnp.cos(angles))
        sine.append(jnp.sin(angles))
    loads[2].wait()
    own = ROWS * HEADS
    part = own // 4
    latent_tiles = KVR // LANES
    blank = jnp.zeros((2 * ROWS, LANES - ROPE), F32)

    units = ROWS // 2
    roped = ((0, 0), (2, 1))
    sizes = [[3 * part if (m, k) in roped else 2 * part for k in range(2)] for m in range(units)]
    starts = [[sum(sum(size) for size in sizes[:m]) + sizes[m][0] * k for k in range(2)] for m in range(units)]

    def unit_rows(m):
        return pl.ds(starts[m][0], sum(sizes[m]))

    def half_of(m, k):
        return pl.ds(starts[m][k], sizes[m][k])

    def rope_rows(w):
        m, k = roped[w]
        return slice(starts[m][k] + 2 * part, starts[m][k] + 3 * part)

    def b_copy(m):
        rows = unit_rows(m)
        return send(b_send.at[rows], q_all.at[c, rows], b_ss.at[m], b_rs.at[m], c, block)

    for w in range(2):

        def add(i, total):
            return total + a_recv[w, lax.rem(c + i, n)].astype(F32)

        arrived(a_recv.at[w, others], a_rs.at[w])
        query = lax.fori_loop(1, n, add, a_send[w, block].astype(F32))
        for u in range(2):
            base = u * HEAD
            nope = query[:, base : base + NOPE].astype(BF16)
            first = query[:, base + NOPE : base + NOPE + half_rope]
            second = query[:, base + NOPE + half_rope : base + HEAD]
            turned = jnp.concatenate(
                [
                    first * cosine[w] - second * sine[w],
                    first * sine[w] + second * cosine[w],
                    blank,
                ],
                axis=1,
            )
            for k in range(4):
                h = 2 * (k ^ w) + u
                here = slice(k * four, (k + 1) * four)
                latent = jnp.dot(nope, wk[h], preferred_element_type=F32)[here]
                place = pl.ds(h, four, stride=HEADS)
                for t in range(latent_tiles):
                    q_rows[w, t, place, :] = latent[:, t * LANES : (t + 1) * LANES]
                q_rows[w, latent_tiles, place, :] = turned[here]
        for u in range(2):
            rows = slice(u * part, (u + 1) * part)
            for t in range(latent_tiles):
                at = starts[2 * w + u][t // 2] + t % 2 * part
                b_send[at : at + part, :] = q_rows[w, t, rows, :].astype(BF16)
        ropes = [
            q_rows[w, latent_tiles, u * part : (u + 1) * part, :][:, :ROPE] for u in range(2)
        ]
        b_send[rope_rows(w), :] = jnp.concatenate(ropes, axis=1).astype(BF16)

        @pl.when(jnp.logical_not(home))
        def _():
            b_copy(2 * w).start()
            b_copy(2 * w + 1).start()

    @pl.when(home)
    def _():
        q_all[c] = b_send[...]

    along = (on_x, on_y)

    def spread(s, m, k, to, sem):
        ref = q_all.at[s, half_of(m, k)]
        go(ref, ref, c_ss.at[0], sem, to, p)

    for m in range(units):

        @pl.when(jnp.logical_not(home))
        def _():
            b_copy(m).wait_recv()

        for i in RING:
            for k in range(2):
                spread(c, m, k, along[k](i), c_rs.at[m, k, SIDE - i])
        for i in RING:
            for k in range(2):
                spread(c, m, k, along[1 - k](i), c_rs.at[m, k, 0])
    for m in range(units):
        for i in RING:
            for k in range(2):
                s = along[k](i)
                arrived(q_all.at[s, half_of(m, k)], c_rs.at[m, k, i])
                for j in RING:
                    spread(s, m, k, along[1 - k](j), c_rs.at[m, k, 0])

    def all_arrived(m):
        for k in range(2):
            arrived(q_all.at[pl.ds(0, SIDE * (SIDE - 1)), half_of(m, k)], c_rs.at[m, k, 0])

    scale = HEAD ** (-0.5)
    heads = n * HEADS
    eye = lax.broadcasted_iota(jnp.int32, (heads, heads), 0) == lax.broadcasted_iota(
        jnp.int32, (heads, heads), 1
    )

    def attend(r, q):
        live = tokens_at[r : r + 1, :] >= 0
        key = keys[r]
        scores = jnp.dot(q, key, preferred_element_type=F32) * scale
        largest = jnp.max(jnp.where(live, scores, -1e30), -1, keepdims=True)
        weights = jnp.where(live, jnp.exp(scores - largest), 0.0)
        total = jnp.sum(weights, -1, keepdims=True)
        summed = lax.dot_general(
            weights.astype(BF16),
            key[:KVR],
            (((1,), (1,)), ((), ())),
            preferred_element_type=F32,
        )
        some = total > 0.0
        safe = jnp.where(some, total, 1.0)
        logs = jnp.where(some, largest + jnp.log(safe), -1e30)
        l_send[r // 2, r % 2 : r % 2 + 1, :] = jnp.sum(jnp.where(eye, logs, 0.0), 0, keepdims=True)
        return summed * (1.0 / safe)

    def pair(m):
        tiles = []
        for t in range(latent_tiles):
            at = starts[m][t // 2] + t % 2 * part
            tiles.append(q_all[:, at : at + part, :])
        tiles.append(q_all[:, rope_rows(m // 2), m % 2 * ROPE : (m % 2 + 1) * ROPE])
        q = jnp.concatenate([tile.astype(F32) for tile in tiles], axis=2)
        first = attend(2 * m, q[:, :HEADS, :].reshape(heads, QK).astype(BF16))
        second = attend(2 * m + 1, q[:, HEADS:, :].reshape(heads, QK).astype(BF16))
        both = jnp.concatenate(
            [first.reshape(n, HEADS, KVR), second.reshape(n, HEADS, KVR)], axis=1
        ).astype(BF16)
        o_send[m] = both.reshape(SIDE, SIDE, part, KVR)

    half_lanes = KVR // 2

    def lanes(k):
        return pl.ds(k * half_lanes, half_lanes)

    def place_of(k, first, second):
        return (first, second) if k == 0 else (second, first)

    me = (x, y)
    three = pl.ds(0, SIDE - 1)

    def slot_of(v, i):
        return lax.rem(v + i, SIDE)

    def send_logs(src, dst, k, m, stage, axis):
        for i in RING:
            go(src, dst.at[k, m, me[axis]], l_ss.at[stage], l_rs.at[k, m, stage], along[axis](i), p)

    def first_stage(m):
        for k in range(2):
            l_first[k, m, me[k]] = l_send[m]
            send_logs(l_send.at[m], l_first, k, m, 0, k)
        for j in RING + (0,):
            for i in RING:
                for k in range(2):
                    to = slot_of(me[1 - k], j)
                    at = place_of(k, slot_of(me[k], i), to)
                    go(
                        o_send.at[m, at[0], at[1], :, lanes(k)],
                        o_first.at[k, m, me[k], to],
                        e_ss.at[0],
                        e_rs.at[k, m, to],
                        along[k](i),
                        p,
                    )

    spot = lax.broadcasted_iota(jnp.int32, (part, heads), 1) - (
        lax.broadcasted_iota(jnp.int32, (part, heads), 0) % HEADS
    )

    def share_column(share, d):
        wide = jnp.broadcast_to(share[:, None, :], (2, HEADS, heads)).reshape(part, heads)
        narrow = jnp.sum(jnp.where(spot == d * HEADS, wide, 0.0), -1, keepdims=True)
        return jnp.broadcast_to(narrow, (part, LANES))

    def scaled(value, share):
        return value.astype(F32) * jnp.concatenate([share] * (half_lanes // LANES), axis=1)

    def shares(buffer, k, m, stage):
        arrived(buffer.at[k, m, three], l_rs.at[k, m, stage])
        logs = buffer[k, m]
        top = jnp.max(logs, 0, keepdims=True)
        raised = jnp.exp(logs - top)
        total = jnp.sum(raised, 0, keepdims=True)
        return raised / total, (top + jnp.log(total))[0]

    def merge(k, m, to):
        at = place_of(k, me[k], to)
        total = scaled(o_send[m, at[0], at[1], :, lanes(k)], l_first_share[k, m, to, me[k]])
        arrived(o_first.at[k, m, three, to], e_rs.at[k, m, to])
        for i in RING:
            s = slot_of(me[k], i)
            total = total + scaled(o_first[k, m, s, to], l_first_share[k, m, to, s])
        return total

    def second_stage(m):
        for k in range(2):
            share, merged = shares(l_first, k, m, 0)
            l_next[k, m] = merged
            l_second[k, m, me[1 - k]] = merged
            send_logs(l_next.at[k, m], l_second, k, m, 1, 1 - k)
            for to in range(SIDE):
                at = place_of(k, me[k], to)
                for s in range(SIDE):
                    l_first_share[k, m, to, s] = share_column(share[s], at[0] * SIDE + at[1])
        for j in RING:
            for k in range(2):
                to = slot_of(me[1 - k], j)
                o_merged[k, m, to] = merge(k, m, to).astype(BF16)
                go(
                    o_merged.at[k, m, to],
                    o_second.at[k, m, me[1 - k]],
                    e_ss.at[1],
                    e_rs.at[k, m, SIDE],
                    along[1 - k](j),
                    p,
                )
        for k in range(2):
            o_kept[k, m] = merge(k, m, me[1 - k])

    def finish(m):
        for k in range(2):
            share, _ = shares(l_second, k, m, 1)
            for s in range(SIDE):
                l_second_share[k, m, s] = share_column(share[s], c)
        for k in range(2):
            total = scaled(o_kept[k, m], l_second_share[k, m, me[1 - k]])
            arrived(o_second.at[k, m, three], e_rs.at[k, m, SIDE])
            for i in RING:
                s = slot_of(me[1 - k], i)
                total = total + scaled(o_second[k, m, s], l_second_share[k, m, s])
            f_send[m, :, lanes(k)] = total.astype(BF16)

    def attention(m):
        all_arrived(m)
        pair(m)
        first_stage(m)

    for m in range(units):
        attention(m)
    for m in range(units):
        second_stage(m)

    def f_copy(w):
        two = pl.ds(2 * w, 2)
        return send(f_send.at[two], f_recv.at[two], f_ss.at[w], f_rs.at[w], c, block)

    for w in range(2):
        for m in (2 * w, 2 * w + 1):
            finish(m)

        @pl.when(jnp.logical_not(home))
        def _():
            f_copy(w).start()

    @pl.when(jnp.logical_not(home))
    def _():
        f_copy(0).wait_recv()
        f_copy(1).wait_recv()

    @pl.when(home)
    def _():
        f_recv[...] = f_send[...]

    per_half = HEADS // 2
    loads[4].wait()
    for m in range(units):
        for t in range(latent_tiles):
            f_rows[t, m * part : (m + 1) * part, :] = f_recv[
                m, :, t * LANES : (t + 1) * LANES
            ].astype(F32)
    values = [
        jnp.dot(
            jnp.concatenate(
                [f_rows[t, pl.ds(h, ROWS, stride=HEADS), :] for t in range(KVR // LANES)], 1
            ).astype(BF16),
            vup[h],
            preferred_element_type=F32,
        )
        for h in range(HEADS)
    ]
    v_all[c] = jnp.concatenate(
        [jnp.concatenate(values[:per_half], 1), jnp.concatenate(values[per_half:], 1)], 0
    ).astype(BF16)

    for k in range(n - 1):
        go(v_all.at[c], v_all.at[c], g_sem.at[0], g_sem.at[1], on_plane(k), p)
    loads[5].wait()
    arrived(v_all.at[others], g_sem.at[1])

    v = v_all[...].astype(F32)
    wide = v.shape[2]
    rows = n * ROWS
    low = v[:, :ROWS, :].reshape(rows, wide).astype(BF16)
    high = v[:, ROWS:, :].reshape(rows, wide).astype(BF16)
    across = (((1,), (1,)), ((), ()))
    result = lax.dot_general(
        low, wo[:, :wide], across, preferred_element_type=F32
    ) + lax.dot_general(high, wo[:, wide:], across, preferred_element_type=F32)
    columns = wo.shape[0]
    cut = h_send.shape[2]
    rest = jnp.concatenate(
        [result[:, cut:], jnp.zeros((rows, 2 * cut - columns), F32)], axis=1
    )
    h_send[...] = jnp.concatenate(
        [result[:, :cut].reshape(n, ROWS, cut), rest.reshape(n, ROWS, cut)], axis=1
    ).astype(BF16)

    own_slot = lax.rem(p + p, n)
    for k in range(n - 1):
        i = n // 2 + (k + 1) // 2 * (1 if k % 2 else -1)
        d = lax.rem(p + i, n)
        go(h_send.at[lax.rem(d + p, n)], h_recv.at[p], h_sem.at[0], h_sem.at[1], c, d)

    def h_add(i, total):
        s = lax.rem(p + i, n)
        return total + h_recv[s].astype(F32)

    arrived(h_recv.at[others], h_sem.at[1])
    summed = lax.fori_loop(1, n, h_add, h_send[own_slot].astype(F32))
    out[...] = jnp.concatenate(
        [summed[:ROWS], summed[ROWS:, : columns - cut]], axis=1
    ).astype(BF16)

    for w in range(2):
        arrived(a_send.at[w, others], a_ss.at[w])
    arrived(q_all.at[others], c_ss.at[0])
    arrived(o_first.at[:, :, three], e_ss.at[0])
    arrived(o_merged.at[:, :, three], e_ss.at[1])
    arrived(l_first.at[:, :, three], l_ss.at[0])
    arrived(l_second.at[:, :, three], l_ss.at[1])
    arrived(v_all.at[others], g_sem.at[0])
    arrived(h_send.at[others], h_sem.at[0])

    @pl.when(jnp.logical_not(home))
    def _():
        for w in range(2):
            f_copy(w).wait_send()
        for m in range(units):
            b_copy(m).wait_send()


def on_device(
    compressed_query,
    query_gain,
    w_query,
    w_key,
    value_up_weight,
    w_output,
    latent_cache,
    context_lengths,
    block_ids,
    block_counts,
):
    n = lax.axis_size("cache")
    rows, rank = compressed_query.shape
    depth, columns = w_query.shape
    span = 256
    w_output = w_output.T
    latent_cache = latent_cache.transpose(0, 2, 1)
    heads = n * HEADS
    own = ROWS * HEADS
    out_columns = w_output.shape[0]
    smem = pl.BlockSpec(memory_space=pltpu.SMEM)
    vmem = pl.BlockSpec(memory_space=pltpu.VMEM)
    hbm = pl.BlockSpec(memory_space=pl.ANY)
    dma = pltpu.SemaphoreType.DMA
    units = ROWS // 2
    chunk = own * QK // LANES
    return pl.pallas_call(
        functools.partial(kernel, n),
        out_shape=jax.ShapeDtypeStruct((ROWS, out_columns), BF16),
        in_specs=[smem, vmem, smem, hbm, vmem, hbm, hbm, hbm, hbm, hbm],
        out_specs=vmem,
        scratch_shapes=[
            pltpu.VMEM((rows, rank), BF16),
            pltpu.VMEM((span, columns), BF16),
            pltpu.VMEM(w_key.shape, BF16),
            pltpu.VMEM(value_up_weight.shape, BF16),
            pltpu.VMEM(w_output.shape, BF16),
            pltpu.VMEM(latent_cache.shape, BF16),
            pltpu.VMEM((ROWS, QK, SLOTS * BLK), BF16),
            pltpu.VMEM((ROWS, SLOTS * BLK), jnp.int32),
            pltpu.VMEM((2, 2, n, ROWS, columns // 4), F32),
            pltpu.VMEM((2, n, 2 * ROWS, columns // 4), BF16),
            pltpu.VMEM((2, n, 2 * ROWS, columns // 4), BF16),
            pltpu.VMEM((2, KVR // LANES + 1, own // 2, LANES), F32),
            pltpu.VMEM((chunk, LANES), BF16),
            pltpu.VMEM((n, chunk, LANES), BF16),
            pltpu.VMEM((units, SIDE, SIDE, 2 * HEADS, KVR), BF16),
            pltpu.VMEM((2, units, SIDE, SIDE, 2 * HEADS, KVR // 2), BF16),
            pltpu.VMEM((2, units, SIDE, 2 * HEADS, KVR // 2), BF16),
            pltpu.VMEM((2, units, SIDE, 2 * HEADS, KVR // 2), BF16),
            pltpu.VMEM((2, units, 2 * HEADS, KVR // 2), F32),
            pltpu.VMEM((units, 2, heads), F32),
            pltpu.VMEM((2, units, SIDE, 2, heads), F32),
            pltpu.VMEM((2, units, SIDE, SIDE, 2 * HEADS, LANES), F32),
            pltpu.VMEM((2, units, SIDE, 2 * HEADS, LANES), F32),
            pltpu.VMEM((2, units, 2, heads), F32),
            pltpu.VMEM((2, units, SIDE, 2, heads), F32),
            pltpu.VMEM((units, 2 * HEADS, KVR), BF16),
            pltpu.VMEM((units, 2 * HEADS, KVR), BF16),
            pltpu.VMEM((KVR // LANES, own, LANES), F32),
            pltpu.VMEM((n, 2 * ROWS, HEADS // 2 * NOPE), BF16),
            pltpu.VMEM((n, 2 * ROWS, 256), BF16),
            pltpu.VMEM((n, 2 * ROWS, 256), BF16),
            dma((6,)),
            dma((2,)),
            dma((2,)),
            dma((units,)),
            dma((units,)),
            dma((1,)),
            dma((units, 2, SIDE)),
            dma((2,)),
            dma((2, units, SIDE + 1)),
            dma((2,)),
            dma((2, units, 2)),
            dma((2,)),
            dma((2,)),
            dma((2,)),
            dma((2,)),
        ],
        compiler_params=pltpu.CompilerParams(
            collective_id=0, has_side_effects=True, vmem_limit_bytes=56 * 2**20
        ),
    )(
        context_lengths,
        block_ids,
        block_counts,
        compressed_query,
        query_gain.reshape(rank // LANES, LANES),
        w_query,
        w_key,
        value_up_weight,
        w_output,
        latent_cache,
    )


def solution(mesh):
    placed = (
        P(),
        P(),
        P("cache", "proj"),
        P("proj", None, None),
        P("proj", None, None),
        P("proj", "cache"),
        P("proj", "cache", None),
        P(),
        P("proj", None),
        P("proj"),
    )
    return jax.shard_map(
        on_device, mesh=mesh, in_specs=placed, out_specs=P("proj", "cache"), check_vma=False
    )
```

```python
import functools

import jax
import jax.numpy as jnp
from jax import lax
from jax.experimental import pallas as pl
from jax.experimental.pallas import tpu as pltpu
from jax.sharding import PartitionSpec as P

NOPE = 128
ROPE = 64
KVR = 512
QK = KVR + ROPE
HEAD = NOPE + ROPE
BLK = 64
SLOTS = 4
ROWS = 8
HEADS = 8
LANES = 128
SIDE = 4
RING = (1, 3, 2)
FAR_FIRST = sorted(
    [(i, j) for i in range(SIDE) for j in range(SIDE) if i or j],
    key=lambda at: -min(at[0], SIDE - at[0]) - min(at[1], SIDE - at[1]),
)
MESH = pl.DeviceIdType.MESH
F32 = jnp.float32
BF16 = jnp.bfloat16


def kernel(
    n,
    lens,
    ids,
    counts,
    cq_hbm,
    gain,
    wq_hbm,
    wk_hbm,
    vup_hbm,
    wo_hbm,
    cache_hbm,
    out,
    cq,
    wq,
    wk,
    vup,
    wo,
    cache,
    keys,
    tokens_at,
    a_pair,
    a_send,
    a_recv,
    q_rows,
    b_send,
    q_all,
    o_send,
    o_first,
    o_merged,
    o_second,
    o_kept,
    l_send,
    l_first,
    l_first_share,
    l_second_share,
    l_next,
    l_second,
    f_send,
    f_recv,
    f_rows,
    v_all,
    h_send,
    h_recv,
    local_sem,
    a_ss,
    a_rs,
    b_ss,
    b_rs,
    c_ss,
    c_rs,
    e_ss,
    e_rs,
    l_ss,
    l_rs,
    f_ss,
    f_rs,
    g_ss,
    g_rs,
    h_sem,
):
    c = lax.axis_index("cache")
    p = lax.axis_index("proj")
    x, y = c // SIDE, lax.rem(c, SIDE)

    def on_x(i):
        return lax.rem(x + i, SIDE) * SIDE + y

    def on_y(i):
        return x * SIDE + lax.rem(y + i, SIDE)

    def on_plane(k):
        dx, dy = FAR_FIRST[k]
        return lax.rem(x + dx, SIDE) * SIDE + lax.rem(y + dy, SIDE)

    def send(src, dst, send_sem, recv_sem, cache_at, proj_at):
        return pltpu.make_async_remote_copy(
            src_ref=src,
            dst_ref=dst,
            send_sem=send_sem,
            recv_sem=recv_sem,
            device_id=(cache_at, proj_at),
            device_id_type=MESH,
        )

    def arrived(ref, sem):
        pltpu.make_async_copy(ref, ref, sem).wait()

    def go(*copy):
        send(*copy).start()

    barrier = pltpu.get_barrier_semaphore()

    def greet(i, carry):
        pl.semaphore_signal(
            barrier, inc=1, device_id=(lax.rem(c + i, n), p), device_id_type=MESH
        )
        pl.semaphore_signal(
            barrier, inc=1, device_id=(c, lax.rem(p + i, n)), device_id_type=MESH
        )
        return carry

    lax.fori_loop(1, n, greet, 0)

    depth = wq_hbm.shape[0]
    width = cq.shape[1]
    span = wq.shape[0]
    start = jnp.minimum((c * depth) // 128 * 128, width - span)
    inside = c * depth - start
    wq[...] = jnp.zeros_like(wq)
    loads = [
        pltpu.make_async_copy(cq_hbm, cq, local_sem.at[0]),
        pltpu.make_async_copy(
            wq_hbm, wq.at[pl.ds(pl.multiple_of(inside, 32), depth)], local_sem.at[1]
        ),
        pltpu.make_async_copy(wk_hbm, wk, local_sem.at[2]),
        pltpu.make_async_copy(cache_hbm, cache, local_sem.at[3]),
        pltpu.make_async_copy(vup_hbm, vup, local_sem.at[4]),
        pltpu.make_async_copy(wo_hbm, wo, local_sem.at[5]),
    ]
    for load in loads:
        load.start()

    loads[0].wait()
    source = cq[...].astype(F32)
    norm = lax.rsqrt(jnp.mean(source * source, -1, keepdims=True) + 1e-06)
    share = pl.ds(pl.multiple_of(start, 128), span)
    tiles = [gain[pl.ds(start // LANES + t, 1), :] for t in range(span // LANES)]
    normed = (cq[:, share].astype(F32) * norm * jnp.concatenate(tiles, 1)).astype(BF16)
    loads[1].wait()
    turned_rows = pltpu.roll(normed.astype(F32).reshape(n, ROWS, span), ROWS // 2, 1)
    turned_rows = turned_rows.reshape(normed.shape).astype(BF16)
    quarter = a_send.shape[3]
    upper = lax.broadcasted_iota(jnp.int32, (n, ROWS, quarter), 1) < ROWS // 2
    for k in range(2):
        even = jnp.dot(
            normed, wq[:, 2 * k * quarter : (2 * k + 1) * quarter], preferred_element_type=F32
        ).reshape(n, ROWS, quarter)
        odd = jnp.dot(
            turned_rows,
            wq[:, (2 * k + 1) * quarter : (2 * k + 2) * quarter],
            preferred_element_type=F32,
        ).reshape(n, ROWS, quarter)
        a_pair[0, k] = jnp.where(upper, even, odd)
        a_pair[1, k] = jnp.where(upper, odd, even)
    for w in range(2):
        a_send[w] = jnp.concatenate([a_pair[w, 0], a_pair[w, 1]], axis=1).astype(BF16)

    pl.semaphore_wait(barrier, 2 * (n - 1))

    for w in range(2):
        for k in range(n - 1):
            d = on_plane(k)
            go(
                a_send.at[w, lax.rem(d + n - p, n)], a_recv.at[w, c], a_ss.at[w], a_rs.at[w], d, p
            )

    ctx_local = cache.shape[2]
    per_shard = ctx_local // BLK
    slots = ids.shape[1]
    tokens = SLOTS * BLK

    def column(ref, base, count=ROWS, repeats=1):
        rows = lax.broadcasted_iota(jnp.int32, (count * repeats, 1), 0)
        found = jnp.zeros((count * repeats, 1), jnp.int32)
        for r in range(count):
            found = jnp.where(rows % count == r, ref[base + r], found)
        return found

    local = ids[...] - c * per_shard
    slot = lax.broadcasted_iota(jnp.int32, (ROWS, slots), 1)
    mine = (slot < column(counts, 0)) & (local >= 0) & (local < per_shard)
    before = lax.broadcasted_iota(jnp.int32, (slots, slots), 0) < lax.broadcasted_iota(
        jnp.int32, (slots, slots), 1
    )
    order = jnp.dot(
        mine.astype(F32), before.astype(F32), preferred_element_type=F32
    )
    lane = lax.broadcasted_iota(jnp.int32, (ROWS, tokens), 1)
    picked = jnp.full((ROWS, tokens), -1, jnp.int32)
    for k in range(SLOTS):
        kept = mine & (order == float(k))
        found = jnp.sum(jnp.where(kept, local + 1, 0), -1, keepdims=True) - 1
        picked = jnp.where(lane // BLK == k, found, picked)
    at = picked * BLK + lane % BLK
    live_at = (picked >= 0) & (c * ctx_local + at < column(lens, p * ROWS))
    tokens_at[...] = jnp.where(live_at, at, -1)

    loads[3].wait()

    def gather(r, carry):
        chosen = lax.broadcasted_iota(jnp.int32, (ctx_local, tokens), 0) == tokens_at[
            pl.ds(r, 1), :
        ]
        keys[r] = jnp.dot(
            cache[r], chosen.astype(F32).astype(BF16), preferred_element_type=F32
        ).astype(BF16)
        return carry

    lax.fori_loop(0, ROWS, gather, 0)

    block = lax.rem(c + n - p, n)
    home = block == p

    others = pl.ds(0, n - 1)
    half_rope = ROPE // 2
    index = lax.broadcasted_iota(jnp.int32, (1, half_rope), 1)
    freq = jnp.zeros((1, half_rope), F32)
    for i in range(half_rope):
        freq = jnp.where(index == i, float(10000.0 ** (-2.0 * i / ROPE)), freq)
    four = ROWS // 2
    cosine, sine = [], []
    for w in range(2):
        angles = (column(lens, block * ROWS + w * four, four, 4) - 1).astype(F32) * freq
        cosine.append(jnp.cos(angles))
        sine.append(jnp.sin(angles))
    loads[2].wait()
    own = ROWS * HEADS
    part = own // 4
    latent_tiles = KVR // LANES
    blank = jnp.zeros((2 * ROWS, LANES - ROPE), F32)

    units = ROWS // 2
    roped = ((0, 0), (2, 1))
    sizes = [[3 * part if (m, k) in roped else 2 * part for k in range(2)] for m in range(units)]
    starts = [[sum(sum(size) for size in sizes[:m]) + sizes[m][0] * k for k in range(2)] for m in range(units)]

    def unit_rows(m):
        return pl.ds(starts[m][0], sum(sizes[m]))

    def half_of(m, k):
        return pl.ds(starts[m][k], sizes[m][k])

    def rope_rows(w):
        m, k = roped[w]
        return slice(starts[m][k] + 2 * part, starts[m][k] + 3 * part)

    def b_copy(m):
        rows = unit_rows(m)
        return send(b_send.at[rows], q_all.at[c, rows], b_ss.at[m], b_rs.at[m], c, block)

    for w in range(2):

        def add(i, total):
            return total + a_recv[w, lax.rem(c + i, n)].astype(F32)

        arrived(a_recv.at[w, others], a_rs.at[w])
        query = lax.fori_loop(1, n, add, a_send[w, block].astype(F32))
        for u in range(2):
            base = u * HEAD
            nope = query[:, base : base + NOPE].astype(BF16)
            first = query[:, base + NOPE : base + NOPE + half_rope]
            second = query[:, base + NOPE + half_rope : base + HEAD]
            turned = jnp.concatenate(
                [
                    first * cosine[w] - second * sine[w],
                    first * sine[w] + second * cosine[w],
                    blank,
                ],
                axis=1,
            )
            for k in range(4):
                h = 2 * (k ^ w) + u
                here = slice(k * four, (k + 1) * four)
                latent = jnp.dot(nope, wk[h], preferred_element_type=F32)[here]
                place = pl.ds(h, four, stride=HEADS)
                for t in range(latent_tiles):
                    q_rows[w, t, place, :] = latent[:, t * LANES : (t + 1) * LANES]
                q_rows[w, latent_tiles, place, :] = turned[here]
        for u in range(2):
            rows = slice(u * part, (u + 1) * part)
            for t in range(latent_tiles):
                at = starts[2 * w + u][t // 2] + t % 2 * part
                b_send[at : at + part, :] = q_rows[w, t, rows, :].astype(BF16)
        ropes = [
            q_rows[w, latent_tiles, u * part : (u + 1) * part, :][:, :ROPE] for u in range(2)
        ]
        b_send[rope_rows(w), :] = jnp.concatenate(ropes, axis=1).astype(BF16)

        @pl.when(jnp.logical_not(home))
        def _():
            b_copy(2 * w).start()
            b_copy(2 * w + 1).start()

    @pl.when(home)
    def _():
        q_all[c] = b_send[...]

    along = (on_x, on_y)

    def spread(s, m, k, to, sem):
        ref = q_all.at[s, half_of(m, k)]
        go(ref, ref, c_ss.at[0], sem, to, p)

    for m in range(units):

        @pl.when(jnp.logical_not(home))
        def _():
            b_copy(m).wait_recv()

        for i in RING:
            for k in range(2):
                spread(c, m, k, along[k](i), c_rs.at[m, k, SIDE - i])
        for i in RING:
            for k in range(2):
                spread(c, m, k, along[1 - k](i), c_rs.at[m, k, 0])
    for m in range(units):
        for i in RING:
            for k in range(2):
                s = along[k](i)
                arrived(q_all.at[s, half_of(m, k)], c_rs.at[m, k, i])
                for j in RING:
                    spread(s, m, k, along[1 - k](j), c_rs.at[m, k, 0])

    def all_arrived(m):
        for k in range(2):
            arrived(q_all.at[pl.ds(0, SIDE * (SIDE - 1)), half_of(m, k)], c_rs.at[m, k, 0])

    scale = HEAD ** (-0.5)
    heads = n * HEADS
    eye = lax.broadcasted_iota(jnp.int32, (heads, heads), 0) == lax.broadcasted_iota(
        jnp.int32, (heads, heads), 1
    )

    def attend(r, q):
        live = tokens_at[r : r + 1, :] >= 0
        key = keys[r]
        scores = jnp.dot(q, key, preferred_element_type=F32) * scale
        largest = jnp.max(jnp.where(live, scores, -1e30), -1, keepdims=True)
        weights = jnp.where(live, jnp.exp(scores - largest), 0.0)
        total = jnp.sum(weights, -1, keepdims=True)
        summed = lax.dot_general(
            weights.astype(BF16),
            key[:KVR],
            (((1,), (1,)), ((), ())),
            preferred_element_type=F32,
        )
        some = total > 0.0
        safe = jnp.where(some, total, 1.0)
        logs = jnp.where(some, largest + jnp.log(safe), -1e30)
        l_send[r // 2, r % 2 : r % 2 + 1, :] = jnp.sum(jnp.where(eye, logs, 0.0), 0, keepdims=True)
        return summed * (1.0 / safe)

    def pair(m):
        tiles = []
        for t in range(latent_tiles):
            at = starts[m][t // 2] + t % 2 * part
            tiles.append(q_all[:, at : at + part, :])
        tiles.append(q_all[:, rope_rows(m // 2), m % 2 * ROPE : (m % 2 + 1) * ROPE])
        q = jnp.concatenate([tile.astype(F32) for tile in tiles], axis=2)
        first = attend(2 * m, q[:, :HEADS, :].reshape(heads, QK).astype(BF16))
        second = attend(2 * m + 1, q[:, HEADS:, :].reshape(heads, QK).astype(BF16))
        both = jnp.concatenate(
            [first.reshape(n, HEADS, KVR), second.reshape(n, HEADS, KVR)], axis=1
        ).astype(BF16)
        o_send[m] = both.reshape(SIDE, SIDE, part, KVR)

    half_lanes = KVR // 2

    def lanes(k):
        return pl.ds(k * half_lanes, half_lanes)

    def place_of(k, first, second):
        return (first, second) if k == 0 else (second, first)

    me = (x, y)
    three = pl.ds(0, SIDE - 1)

    def slot_of(v, i):
        return lax.rem(v + i, SIDE)

    def send_logs(src, dst, k, m, stage, axis):
        for i in RING:
            go(src, dst.at[k, m, me[axis]], l_ss.at[stage], l_rs.at[k, m, stage], along[axis](i), p)

    def first_stage(m):
        for k in range(2):
            l_first[k, m, me[k]] = l_send[m]
            send_logs(l_send.at[m], l_first, k, m, 0, k)
        for j in RING + (0,):
            for i in RING:
                for k in range(2):
                    to = slot_of(me[1 - k], j)
                    at = place_of(k, slot_of(me[k], i), to)
                    go(
                        o_send.at[m, at[0], at[1], :, lanes(k)],
                        o_first.at[k, m, me[k], to],
                        e_ss.at[0],
                        e_rs.at[k, m, to],
                        along[k](i),
                        p,
                    )

    spot = lax.broadcasted_iota(jnp.int32, (part, heads), 1) - (
        lax.broadcasted_iota(jnp.int32, (part, heads), 0) % HEADS
    )

    def share_column(share, d):
        wide = jnp.broadcast_to(share[:, None, :], (2, HEADS, heads)).reshape(part, heads)
        narrow = jnp.sum(jnp.where(spot == d * HEADS, wide, 0.0), -1, keepdims=True)
        return jnp.broadcast_to(narrow, (part, LANES))

    def scaled(value, share):
        return value.astype(F32) * jnp.concatenate([share] * (half_lanes // LANES), axis=1)

    def shares(buffer, k, m, stage):
        arrived(buffer.at[k, m, three], l_rs.at[k, m, stage])
        logs = buffer[k, m]
        top = jnp.max(logs, 0, keepdims=True)
        raised = jnp.exp(logs - top)
        total = jnp.sum(raised, 0, keepdims=True)
        return raised / total, (top + jnp.log(total))[0]

    def merge(k, m, to):
        at = place_of(k, me[k], to)
        total = scaled(o_send[m, at[0], at[1], :, lanes(k)], l_first_share[k, m, to, me[k]])
        arrived(o_first.at[k, m, three, to], e_rs.at[k, m, to])
        for i in RING:
            s = slot_of(me[k], i)
            total = total + scaled(o_first[k, m, s, to], l_first_share[k, m, to, s])
        return total

    def second_stage(m):
        for k in range(2):
            share, merged = shares(l_first, k, m, 0)
            l_next[k, m] = merged
            l_second[k, m, me[1 - k]] = merged
            send_logs(l_next.at[k, m], l_second, k, m, 1, 1 - k)
            for to in range(SIDE):
                at = place_of(k, me[k], to)
                for s in range(SIDE):
                    l_first_share[k, m, to, s] = share_column(share[s], at[0] * SIDE + at[1])
        for j in RING:
            for k in range(2):
                to = slot_of(me[1 - k], j)
                o_merged[k, m, to] = merge(k, m, to).astype(BF16)
                go(
                    o_merged.at[k, m, to],
                    o_second.at[k, m, me[1 - k]],
                    e_ss.at[1],
                    e_rs.at[k, m, SIDE],
                    along[1 - k](j),
                    p,
                )
        for k in range(2):
            o_kept[k, m] = merge(k, m, me[1 - k])

    def finish(m):
        for k in range(2):
            share, _ = shares(l_second, k, m, 1)
            for s in range(SIDE):
                l_second_share[k, m, s] = share_column(share[s], c)
        for k in range(2):
            total = scaled(o_kept[k, m], l_second_share[k, m, me[1 - k]])
            arrived(o_second.at[k, m, three], e_rs.at[k, m, SIDE])
            for i in RING:
                s = slot_of(me[1 - k], i)
                total = total + scaled(o_second[k, m, s], l_second_share[k, m, s])
            f_send[m, :, lanes(k)] = total.astype(BF16)

    def attention(m):
        all_arrived(m)
        pair(m)
        first_stage(m)

    for m in range(units):
        attention(m)
    for m in range(units):
        second_stage(m)

    def f_copy(m):
        return send(f_send.at[m], f_recv.at[m], f_ss.at[m], f_rs.at[m], c, block)

    for m in range(units):
        finish(m)

        @pl.when(jnp.logical_not(home))
        def _():
            f_copy(m).start()

    @pl.when(home)
    def _():
        f_recv[...] = f_send[...]

    loads[4].wait()
    for w in range(2):

        @pl.when(jnp.logical_not(home))
        def _():
            f_copy(2 * w).wait_recv()
            f_copy(2 * w + 1).wait_recv()

        for u in range(2):
            for t in range(latent_tiles):
                f_rows[w, t, u * part : (u + 1) * part, :] = f_recv[
                    2 * w + u, :, t * LANES : (t + 1) * LANES
                ].astype(F32)
        values = []
        for h in range(HEADS):
            row_tiles = [
                f_rows[w, t, pl.ds(h, four, stride=HEADS), :] for t in range(latent_tiles)
            ]
            values.append(
                jnp.dot(
                    jnp.concatenate(row_tiles, 1).astype(BF16),
                    vup[h],
                    preferred_element_type=F32,
                )
            )
        quarters = [
            jnp.concatenate([values[2 * (k ^ w)], values[2 * (k ^ w) + 1]], 1) for k in range(4)
        ]
        v_all[w, c] = jnp.concatenate(quarters, 0).astype(BF16)
        for k in range(n - 1):
            go(v_all.at[w, c], v_all.at[w, c], g_ss.at[w], g_rs.at[w], on_plane(k), p)
    loads[5].wait()
    for w in range(2):
        arrived(v_all.at[w, others], g_rs.at[w])

    wide = v_all.shape[3]
    rows = n * ROWS
    above = lax.broadcasted_iota(jnp.int32, (n, ROWS, wide), 1) < four
    across = (((1,), (1,)), ((), ()))
    result = None
    for k in range(2):
        early = v_all[0, :, k * ROWS : (k + 1) * ROWS, :].astype(F32)
        late = v_all[1, :, k * ROWS : (k + 1) * ROWS, :].astype(F32)
        even = jnp.where(above, early, late)
        odd = pltpu.roll(jnp.where(above, late, early), four, 1)
        both = jnp.concatenate([even.reshape(rows, wide), odd.reshape(rows, wide)], 1).astype(BF16)
        term = lax.dot_general(
            both,
            wo[:, 2 * k * wide : 2 * (k + 1) * wide],
            across,
            preferred_element_type=F32,
        )
        result = term if result is None else result + term
    columns = wo.shape[0]
    cut = h_send.shape[2]
    rest = jnp.concatenate(
        [result[:, cut:], jnp.zeros((rows, 2 * cut - columns), F32)], axis=1
    )
    h_send[...] = jnp.concatenate(
        [result[:, :cut].reshape(n, ROWS, cut), rest.reshape(n, ROWS, cut)], axis=1
    ).astype(BF16)

    own_slot = lax.rem(p + p, n)
    for k in range(n - 1):
        i = n // 2 + (k + 1) // 2 * (1 if k % 2 else -1)
        d = lax.rem(p + i, n)
        go(h_send.at[lax.rem(d + p, n)], h_recv.at[p], h_sem.at[0], h_sem.at[1], c, d)

    def h_add(i, total):
        s = lax.rem(p + i, n)
        return total + h_recv[s].astype(F32)

    arrived(h_recv.at[others], h_sem.at[1])
    summed = lax.fori_loop(1, n, h_add, h_send[own_slot].astype(F32))
    out[...] = jnp.concatenate(
        [summed[:ROWS], summed[ROWS:, : columns - cut]], axis=1
    ).astype(BF16)

    for w in range(2):
        arrived(a_send.at[w, others], a_ss.at[w])
    arrived(q_all.at[others], c_ss.at[0])
    arrived(o_first.at[:, :, three], e_ss.at[0])
    arrived(o_merged.at[:, :, three], e_ss.at[1])
    arrived(l_first.at[:, :, three], l_ss.at[0])
    arrived(l_second.at[:, :, three], l_ss.at[1])
    for w in range(2):
        arrived(v_all.at[w, others], g_ss.at[w])
    arrived(h_send.at[others], h_sem.at[0])

    @pl.when(jnp.logical_not(home))
    def _():
        for m in range(units):
            b_copy(m).wait_send()
            f_copy(m).wait_send()


def on_device(
    compressed_query,
    query_gain,
    w_query,
    w_key,
    value_up_weight,
    w_output,
    latent_cache,
    context_lengths,
    block_ids,
    block_counts,
):
    n = lax.axis_size("cache")
    rows, rank = compressed_query.shape
    depth, columns = w_query.shape
    span = 256
    w_output = w_output.T
    latent_cache = latent_cache.transpose(0, 2, 1)
    heads = n * HEADS
    own = ROWS * HEADS
    out_columns = w_output.shape[0]
    smem = pl.BlockSpec(memory_space=pltpu.SMEM)
    vmem = pl.BlockSpec(memory_space=pltpu.VMEM)
    hbm = pl.BlockSpec(memory_space=pl.ANY)
    dma = pltpu.SemaphoreType.DMA
    units = ROWS // 2
    chunk = own * QK // LANES
    return pl.pallas_call(
        functools.partial(kernel, n),
        out_shape=jax.ShapeDtypeStruct((ROWS, out_columns), BF16),
        in_specs=[smem, vmem, smem, hbm, vmem, hbm, hbm, hbm, hbm, hbm],
        out_specs=vmem,
        scratch_shapes=[
            pltpu.VMEM((rows, rank), BF16),
            pltpu.VMEM((span, columns), BF16),
            pltpu.VMEM(w_key.shape, BF16),
            pltpu.VMEM(value_up_weight.shape, BF16),
            pltpu.VMEM(w_output.shape, BF16),
            pltpu.VMEM(latent_cache.shape, BF16),
            pltpu.VMEM((ROWS, QK, SLOTS * BLK), BF16),
            pltpu.VMEM((ROWS, SLOTS * BLK), jnp.int32),
            pltpu.VMEM((2, 2, n, ROWS, columns // 4), F32),
            pltpu.VMEM((2, n, 2 * ROWS, columns // 4), BF16),
            pltpu.VMEM((2, n, 2 * ROWS, columns // 4), BF16),
            pltpu.VMEM((2, KVR // LANES + 1, own // 2, LANES), F32),
            pltpu.VMEM((chunk, LANES), BF16),
            pltpu.VMEM((n, chunk, LANES), BF16),
            pltpu.VMEM((units, SIDE, SIDE, 2 * HEADS, KVR), BF16),
            pltpu.VMEM((2, units, SIDE, SIDE, 2 * HEADS, KVR // 2), BF16),
            pltpu.VMEM((2, units, SIDE, 2 * HEADS, KVR // 2), BF16),
            pltpu.VMEM((2, units, SIDE, 2 * HEADS, KVR // 2), BF16),
            pltpu.VMEM((2, units, 2 * HEADS, KVR // 2), F32),
            pltpu.VMEM((units, 2, heads), F32),
            pltpu.VMEM((2, units, SIDE, 2, heads), F32),
            pltpu.VMEM((2, units, SIDE, SIDE, 2 * HEADS, LANES), F32),
            pltpu.VMEM((2, units, SIDE, 2 * HEADS, LANES), F32),
            pltpu.VMEM((2, units, 2, heads), F32),
            pltpu.VMEM((2, units, SIDE, 2, heads), F32),
            pltpu.VMEM((units, 2 * HEADS, KVR), BF16),
            pltpu.VMEM((units, 2 * HEADS, KVR), BF16),
            pltpu.VMEM((2, KVR // LANES, own // 2, LANES), F32),
            pltpu.VMEM((2, n, 2 * ROWS, HEADS // 4 * NOPE), BF16),
            pltpu.VMEM((n, 2 * ROWS, 256), BF16),
            pltpu.VMEM((n, 2 * ROWS, 256), BF16),
            dma((6,)),
            dma((2,)),
            dma((2,)),
            dma((units,)),
            dma((units,)),
            dma((1,)),
            dma((units, 2, SIDE)),
            dma((2,)),
            dma((2, units, SIDE + 1)),
            dma((2,)),
            dma((2, units, 2)),
            dma((units,)),
            dma((units,)),
            dma((2,)),
            dma((2,)),
            dma((2,)),
        ],
        compiler_params=pltpu.CompilerParams(
            collective_id=0, has_side_effects=True, vmem_limit_bytes=56 * 2**20
        ),
    )(
        context_lengths,
        block_ids,
        block_counts,
        compressed_query,
        query_gain.reshape(rank // LANES, LANES),
        w_query,
        w_key,
        value_up_weight,
        w_output,
        latent_cache,
    )


def solution(mesh):
    placed = (
        P(),
        P(),
        P("cache", "proj"),
        P("proj", None, None),
        P("proj", None, None),
        P("proj", "cache"),
        P("proj", "cache", None),
        P(),
        P("proj", None),
        P("proj"),
    )
    return jax.shard_map(
        on_device, mesh=mesh, in_specs=placed, out_specs=P("proj", "cache"), check_vma=False
    )
```
